32 devices in a mesh: dp: 32 (over z, y, x, core).
Axes of the slice: x: 2, y: 2, z: 4, core: 2. Of those that a mesh axis runs over, the one named last changes fastest.
Arguments:
- tokens: bfloat16 [32, 320, 768], P('dp'), may hold values from -6 to 6
- latents: float32 [32, 256, 16], P('dp'), may hold values from -30 to 30
- orders: int32 [32, 256], P('dp'), may hold values from 0 to 255, each once within a row
- counts: int32 [32], P('dp'), may hold values from 179 to 256, as said below
- timesteps: int32 [8192, 4], P('dp'), may hold values from 0 to 999
- noise: float32 [8192, 4, 16], P('dp'), may hold values from -6 to 6
- enc_gain1: bfloat16 [768], P('dp'), may hold values from 0.5 to 1.5
- enc_bias1: bfloat16 [768], P('dp'), may hold values from -1 to 1
- enc_qkv: bfloat16 [768, 2304], P('dp'), may hold values from -0.21875 to 0.21875
- enc_proj: bfloat16 [768, 768], P('dp'), may hold values from -0.875 to 0.875
- enc_gain2: bfloat16 [768], P('dp'), may hold values from 0.5 to 1.5
- enc_bias2: bfloat16 [768], P('dp'), may hold values from -1 to 1
- enc_fc1: bfloat16 [768, 3072], P('dp'), may hold values from -0.21875 to 0.21875
- enc_fc2: bfloat16 [3072, 768], P('dp'), may hold values from -0.109375 to 0.109375
- dec_gain1: bfloat16 [768], P('dp'), may hold values from 0.5 to 1.5
- dec_bias1: bfloat16 [768], P('dp'), may hold values from -1 to 1
- dec_qkv: bfloat16 [768, 2304], P('dp'), may hold values from -0.21875 to 0.21875
- dec_proj: bfloat16 [768, 768], P('dp'), may hold values from -0.875 to 0.875
- dec_gain2: bfloat16 [768], P('dp'), may hold values from 0.5 to 1.5
- dec_bias2: bfloat16 [768], P('dp'), may hold values from -1 to 1
- dec_fc1: bfloat16 [768, 3072], P('dp'), may hold values from -0.21875 to 0.21875
- dec_fc2: bfloat16 [3072, 768], P('dp'), may hold values from -0.109375 to 0.109375
- mask_token: bfloat16 [768], P('dp'), may hold values from -4 to 4
- diff_in: bfloat16 [16, 1024], P(None, 'dp'), may hold values from -1.5 to 1.5
- diff_time1: bfloat16 [256, 1024], P('dp'), may hold values from -0.375 to 0.375
- diff_time2: bfloat16 [1024, 1024], P('dp'), may hold values from -0.1875 to 0.1875
- diff_cond: bfloat16 [768, 1024], P('dp'), may hold values from -0.21875 to 0.21875
- diff_ada: bfloat16 [1024, 3072], P('dp'), may hold values from -0.1875 to 0.1875
- diff_mlp1: bfloat16 [1024, 1024], P('dp'), may hold values from -0.1875 to 0.1875
- diff_mlp2: bfloat16 [1024, 1024], P('dp'), may hold values from -0.1875 to 0.1875
- diff_final: bfloat16 [1024, 2048], P('dp'), may hold values from -0.1875 to 0.1875
- diff_out: bfloat16 [1024, 16], P('dp'), may hold values from -0.1875 to 0.1875
Outputs:
- loss_mean: float32 [], replicated
- grad_tokens: float32 [32, 320, 768], P('dp')
- grad_enc_gain1: float32 [768], P('dp')
- grad_enc_bias1: float32 [768], P('dp')
- grad_enc_qkv: float32 [768, 2304], P('dp')
- grad_enc_proj: float32 [768, 768], P('dp')
- grad_enc_gain2: float32 [768], P('dp')
- grad_enc_bias2: float32 [768], P('dp')
- grad_enc_fc1: float32 [768, 3072], P('dp')
- grad_enc_fc2: float32 [3072, 768], P('dp')
- grad_dec_gain1: float32 [768], P('dp')
- grad_dec_bias1: float32 [768], P('dp')
- grad_dec_qkv: float32 [768, 2304], P('dp')
- grad_dec_proj: float32 [768, 768], P('dp')
- grad_dec_gain2: float32 [768], P('dp')
- grad_dec_bias2: float32 [768], P('dp')
- grad_dec_fc1: float32 [768, 3072], P('dp')
- grad_dec_fc2: float32 [3072, 768], P('dp')
- grad_mask_token: float32 [768], P('dp')
- grad_diff_in: float32 [16, 1024], P(None, 'dp')
- grad_diff_time1: float32 [256, 1024], P('dp')
- grad_diff_time2: float32 [1024, 1024], P('dp')
- grad_diff_cond: float32 [768, 1024], P('dp')
- grad_diff_ada: float32 [1024, 3072], P('dp')
- grad_diff_mlp1: float32 [1024, 1024], P('dp')
- grad_diff_mlp2: float32 [1024, 1024], P('dp')
- grad_diff_final: float32 [1024, 2048], P('dp')
- grad_diff_out: float32 [1024, 16], P('dp')
The draws below stay inside these ranges and needn't reach their ends.
Inputs may be any that keep to these rules, and one draw needn't show every extreme that they name: `orders`: each image's row is a permutation of 0 to 255. `counts`: in every draw some image has 179 and some image has 256.
All inputs are finite; a program needn't handle non-finite values.
Results may differ from the reference program's by a relative error of at most 0.02.
Values may be sent and summed in bfloat16 or wider, within the bound.
No kernel may reach another device: no remote copies, remote signals or barrier semaphores. Data moves between devices by JAX's collectives and lax.ppermute only.
A program may use at most 384 MiB of HBM per device.

```python
import math
import jax
import jax.numpy as jnp
from jax import lax

D = 768
HEAD = 64
FF = 3072
WD = 1024
CH = 16
FREQ = 256
BUF = 64
L = 256
COPIES = 4
CMIN = 179
IMG_DEV = 1
S = 320
IMAGES = 32
SLOT = 8
RECV = 256
RECV_ALL = 8192
N_DP = 32


def draw_latents(key, part):
    key = jax.random.fold_in(key, 11)
    centre_key, fluct_key, spread_key = jax.random.split(key, 3)
    ramp_rows = 1.0 + 2.0 * jnp.arange(IMAGES, dtype=jnp.float32) / (IMAGES - 1)
    centre = jax.random.uniform(centre_key, (CH,), jnp.float32, -1.5, 1.5)
    spread = jax.random.uniform(spread_key, (CH,), jnp.float32, 0.5, 2.0)
    fluctuation = jnp.clip(jax.random.normal(fluct_key, (IMAGES, L, CH), jnp.float32), -4.0, 4.0)
    return (centre[None, None, :] + spread[None, None, :] * fluctuation) * ramp_rows[:, None, None]


def draw_counts(key, part):
    key = jax.random.fold_in(key, 12)
    value_key, place_key = jax.random.split(key)
    counts_drawn = jax.random.randint(value_key, (IMAGES,), CMIN, L + 1, dtype=jnp.int32)
    chosen = jax.random.permutation(place_key, IMAGES)
    counts_drawn = counts_drawn.at[chosen[0]].set(L)
    return counts_drawn.at[chosen[1]].set(CMIN)


def place_ends(values, key, smallest, high):
    index_at = [jax.random.randint(jax.random.fold_in(key, axis), (), 0, length) for axis, length in enumerate(values.shape)]
    widest = values.shape.index(max(values.shape))
    neighbour = index_at[:widest] + [(index_at[widest] + 1) % values.shape[widest]] + index_at[widest + 1:]
    return values.at[tuple(index_at)].set(smallest).at[tuple(neighbour)].set(high)


def level_of(stream_key, shape, shards, smallest, high):
    factor_of = 1.0
    for position, shards_of in shards:
        steps = jax.random.uniform(jax.random.fold_in(jax.random.fold_in(stream_key, 6), position), (shards_of,), jnp.float32, smallest / len(shards), high / len(shards))
        factor_of = factor_of * jnp.repeat(jnp.exp(steps), shape[position] // shards_of).reshape((-1,) + (1,) * (len(shape) - 1 - position))
    return factor_of


def bell_draw(key, dims, scale, most, shards=(), kind=jnp.bfloat16):
    entries = scale * jax.random.normal(key, dims, jnp.float32)
    if shards:
        entries = entries * level_of(key, dims, shards, -0.22, 0.18)
    return jnp.clip(entries, -most, most).astype(kind)


def setup_inputs(seed: int = 0) -> dict:
    seeds = jax.random.split(jax.random.key(seed), 33)
    return {
        "tokens": bell_draw(seeds[0], (IMAGES, S, D), 1.0, 6.0, ((0, 32),)),
        "latents": draw_latents(jax.random.fold_in(seeds[32], 71), 0),
        "orders": jax.vmap(lambda own: jax.random.permutation(own, L))(jax.random.split(seeds[2], IMAGES)).reshape((IMAGES, L)).astype(jnp.int32),
        "counts": draw_counts(jax.random.fold_in(seeds[32], 71), 0),
        "timesteps": place_ends(jax.random.randint(seeds[4], (RECV_ALL, COPIES), 0, 1000), jax.random.fold_in(seeds[4], 1), 0, 999).astype(jnp.int32),
        "noise": bell_draw(seeds[5], (RECV_ALL, COPIES, CH), 1.0, 6.0, ((0, 32),), jnp.float32),
        "enc_gain1": jnp.clip(1.0 + 0.1 * jax.random.normal(seeds[6], (D,), jnp.float32), 0.5, 1.5).astype(jnp.bfloat16),
        "enc_bias1": bell_draw(seeds[7], (D,), 0.2, 1.0, ((0, 32),)),
        "enc_qkv": bell_draw(seeds[8], (D, 3 * D), D ** -0.5, 0.21875, ((0, 32),)),
        "enc_proj": bell_draw(seeds[9], (D, D), (D // 16) ** -0.5, 0.875, ((0, 32),)),
        "enc_gain2": jnp.clip(1.0 + 0.1 * jax.random.normal(seeds[10], (D,), jnp.float32), 0.5, 1.5).astype(jnp.bfloat16),
        "enc_bias2": bell_draw(seeds[11], (D,), 0.2, 1.0, ((0, 32),)),
        "enc_fc1": bell_draw(seeds[12], (D, FF), D ** -0.5, 0.21875, ((0, 32),)),
        "enc_fc2": bell_draw(seeds[13], (FF, D), FF ** -0.5, 0.109375, ((0, 32),)),
        "dec_gain1": jnp.clip(1.0 + 0.1 * jax.random.normal(seeds[14], (D,), jnp.float32), 0.5, 1.5).astype(jnp.bfloat16),
        "dec_bias1": bell_draw(seeds[15], (D,), 0.2, 1.0, ((0, 32),)),
        "dec_qkv": bell_draw(seeds[16], (D, 3 * D), D ** -0.5, 0.21875, ((0, 32),)),
        "dec_proj": bell_draw(seeds[17], (D, D), (D // 16) ** -0.5, 0.875, ((0, 32),)),
        "dec_gain2": jnp.clip(1.0 + 0.1 * jax.random.normal(seeds[18], (D,), jnp.float32), 0.5, 1.5).astype(jnp.bfloat16),
        "dec_bias2": bell_draw(seeds[19], (D,), 0.2, 1.0, ((0, 32),)),
        "dec_fc1": bell_draw(seeds[20], (D, FF), D ** -0.5, 0.21875, ((0, 32),)),
        "dec_fc2": bell_draw(seeds[21], (FF, D), FF ** -0.5, 0.109375, ((0, 32),)),
        "mask_token": bell_draw(seeds[22], (D,), 1.0, 4.0, ((0, 32),)),
        "diff_in": bell_draw(seeds[23], (CH, WD), CH ** -0.5, 1.5, ((1, 32),)),
        "diff_time1": bell_draw(seeds[24], (FREQ, WD), FREQ ** -0.5, 0.375, ((0, 32),)),
        "diff_time2": bell_draw(seeds[25], (WD, WD), WD ** -0.5, 0.1875, ((0, 32),)),
        "diff_cond": bell_draw(seeds[26], (D, WD), D ** -0.5, 0.21875, ((0, 32),)),
        "diff_ada": bell_draw(seeds[27], (WD, 3 * WD), WD ** -0.5, 0.1875, ((0, 32),)),
        "diff_mlp1": bell_draw(seeds[28], (WD, WD), WD ** -0.5, 0.1875, ((0, 32),)),
        "diff_mlp2": bell_draw(seeds[29], (WD, WD), WD ** -0.5, 0.1875, ((0, 32),)),
        "diff_final": bell_draw(seeds[30], (WD, 2 * WD), WD ** -0.5, 0.1875, ((0, 32),)),
        "diff_out": bell_draw(seeds[31], (WD, CH), WD ** -0.5, 0.1875, ((0, 32),)),
    }


@jax.custom_vjp
def low(v):
    return lax.optimization_barrier(v.astype(jnp.bfloat16)).astype(jnp.float32)

@jax.custom_vjp
def low_back(v):
    return v

def low_keep(v):
    return (low(v), None)

def low_pass(kept, grad):
    return (grad,)

def back_keep(v):
    return (v, None)

def back_low(kept, grad):
    return (low(grad),)
low.defvjp(low_keep, low_pass)
low_back.defvjp(back_keep, back_low)

def product(left, right):
    return jnp.dot(left, right, precision=lax.Precision.HIGHEST)

def layer_norm(residual, gain, offset):
    centred = residual - lax.optimization_barrier(jnp.mean(residual, axis=-1, keepdims=True))
    spread = lax.optimization_barrier(jnp.mean(centred * centred, axis=-1, keepdims=True))
    return centred * lax.rsqrt(spread + 1e-06) * gain + offset

def plain_norm(residual):
    centred = residual - lax.optimization_barrier(jnp.mean(residual, axis=-1, keepdims=True))
    spread = lax.optimization_barrier(jnp.mean(centred * centred, axis=-1, keepdims=True))
    return centred * lax.rsqrt(spread + 1e-06)

def residual_block(residual, keys_live, weights):
    gain1, offset1, qkv_w, proj_w, gain2, offset2, fc1_w, fc2_w = weights
    groups = residual.shape[0]
    positions = residual.shape[1]
    model_width = residual.shape[2]
    head_count = model_width // HEAD
    highest = lax.Precision.HIGHEST
    normed = low(layer_norm(residual, gain1, offset1))
    projected = low(low_back(jnp.einsum('gsd,de->gse', normed, qkv_w, precision=highest)))
    projected = projected.reshape(groups, positions, 3, head_count, HEAD)
    query_rows = projected[:, :, 0]
    key_rows = projected[:, :, 1]
    value_rows = projected[:, :, 2]
    scores = low_back(jnp.einsum('gqhe,gkhe->ghqk', query_rows, key_rows, precision=highest) * HEAD ** (-0.5))
    scores = jnp.where(keys_live[:, None, None, :], scores, -1e+30)
    soft_rounded = low(jax.nn.softmax(scores, axis=-1))
    attended = low(low_back(jnp.einsum('ghqk,gkhe->gqhe', soft_rounded, value_rows, precision=highest)))
    attended = attended.reshape(groups, positions, model_width)
    middle = residual + low_back(jnp.einsum('gsd,de->gse', attended, proj_w, precision=highest))
    normed_second = low(layer_norm(middle, gain2, offset2))
    hidden = low_back(jnp.einsum('gsd,df->gsf', normed_second, fc1_w, precision=highest))
    active = low(jax.nn.gelu(hidden, approximate=False))
    return middle + low_back(jnp.einsum('gsf,fd->gsd', active, fc2_w, precision=highest))

def transform_group(enc_params, dec_params, mask_vector, tokens_group, masked_group):
    group_size = tokens_group.shape[0]
    live_keys = jnp.concatenate([jnp.ones((group_size, BUF), jnp.int32), 1 - masked_group], axis=1) > 0
    encoded = residual_block(tokens_group, live_keys, enc_params)
    decoder_in = jnp.where(live_keys[:, :, None], encoded, mask_vector[None, None, :])
    decoded = residual_block(decoder_in, jnp.ones_like(live_keys), dec_params)
    return low(low_back(decoded[:, BUF:]))

def modulate(residual, shift_part, scale_part):
    return plain_norm(residual) * (1.0 + scale_part) + shift_part

def diffuse(diff_params, cond_rows, target_rows, noise_rows, step_rows, live_rows):
    in_w, time1_w, time2_w, cond_w, ada_w, mlp1_w, mlp2_w, final_w, out_w = diff_params
    count_rows = cond_rows.shape[0]
    copies = noise_rows.shape[1]
    flat_rows = count_rows * copies
    inner_width = in_w.shape[1]
    steps_float = step_rows.astype(jnp.float32)
    angle_noise = (steps_float / 1000.0 + 0.008) / 1.008 * (math.pi / 2)
    keep_part = jnp.cos(angle_noise) ** 2
    noisy_rows = jnp.sqrt(keep_part)[:, :, None] * target_rows[:, None, :] + jnp.sqrt(1.0 - keep_part)[:, :, None] * noise_rows
    start_rows = low_back(product(low(noisy_rows.reshape(flat_rows, CH)), in_w))
    half_freq = FREQ // 2
    frequency = jnp.exp(-math.log(10000.0) * jnp.arange(half_freq, dtype=jnp.float32) / half_freq)
    phases = steps_float.reshape(flat_rows, 1) * frequency[None, :]
    sinusoid = low(jnp.concatenate([jnp.cos(phases), jnp.sin(phases)], axis=1))
    time_pre = low_back(product(sinusoid, time1_w))
    time_emb = low_back(product(low(jax.nn.silu(time_pre)), time2_w))
    cond_emb = low_back(product(cond_rows, cond_w))
    context = time_emb.reshape(count_rows, copies, inner_width) + cond_emb[:, None, :]
    context = low(jax.nn.silu(context)).reshape(flat_rows, inner_width)
    modulation = low_back(product(context, ada_w))
    shift_first = modulation[:, :inner_width]
    scale_first = modulation[:, inner_width:2 * inner_width]
    gate_first = modulation[:, 2 * inner_width:]
    first_in = low(modulate(start_rows, shift_first, scale_first))
    first_pre = low_back(product(first_in, mlp1_w))
    branch = low_back(product(low(jax.nn.silu(first_pre)), mlp2_w))
    middle = start_rows + gate_first * branch
    final_mod = low_back(product(context, final_w))
    final_in = low(modulate(middle, final_mod[:, :inner_width], final_mod[:, inner_width:]))
    output = low_back(product(final_in, out_w))
    residue = output.reshape(count_rows, copies, CH) - noise_rows
    return jnp.sum(live_rows[:, None, None] * residue * residue) / (copies * CH)

def reference(tokens, latents, orders, counts, timesteps, noise, enc_gain1, enc_bias1, enc_qkv, enc_proj, enc_gain2, enc_bias2, enc_fc1, enc_fc2, dec_gain1, dec_bias1, dec_qkv, dec_proj, dec_gain2, dec_bias2, dec_fc1, dec_fc2, mask_token, diff_in, diff_time1, diff_time2, diff_cond, diff_ada, diff_mlp1, diff_mlp2, diff_final, diff_out):
    cell_count = IMAGES * L
    flat_latents = latents.reshape(cell_count, CH)
    average = lax.optimization_barrier(jnp.sum(flat_latents, axis=0)) / cell_count
    spread = lax.optimization_barrier(jnp.sum(flat_latents * flat_latents, axis=0)) / cell_count - average * average
    target = low((flat_latents - average) * lax.rsqrt(spread + 1e-06))
    total = jnp.sum(counts).astype(jnp.float32)
    masked = (orders < counts[:, None]).astype(jnp.int32)
    per_device = masked.reshape(N_DP, IMG_DEV * L)
    rank_rows = jnp.cumsum(per_device, axis=1) - per_device
    anchor = jnp.arange(N_DP, dtype=jnp.int32)[:, None]
    global_slot = rank_rows % N_DP * RECV + anchor * SLOT + rank_rows // N_DP
    global_slot = jnp.where(per_device > 0, global_slot, 0).reshape(cell_count).astype(jnp.int32)
    row_noise = noise[global_slot]
    row_steps = timesteps[global_slot]
    live_rows = masked.reshape(cell_count).astype(jnp.float32)
    block_count = cell_count // 1024
    target_blocks = target.reshape(block_count, 1024, CH)
    noise_blocks = row_noise.reshape(block_count, 1024, COPIES, CH)
    step_blocks = row_steps.reshape(block_count, 1024, COPIES)
    live_blocks = live_rows.reshape(block_count, 1024)
    masked_groups = masked.reshape(IMAGES // 8, 8, L)

    def objective(enc_params, dec_params, mask_vector, diff_params, tokens_full):
        grouped = tokens_full.reshape(IMAGES // 8, 8, S, D)

        def group_pass(pieces):
            return transform_group(enc_params, dec_params, mask_vector, pieces[0], pieces[1])
        conds = lax.map(jax.checkpoint(group_pass), (grouped, masked_groups))
        cond_blocks = conds.reshape(block_count, 1024, D)

        def block_loss(pieces):
            return diffuse(diff_params, pieces[0], pieces[1], pieces[2], pieces[3], pieces[4])
        totals = lax.map(jax.checkpoint(block_loss), (cond_blocks, target_blocks, noise_blocks, step_blocks, live_blocks))
        return jnp.sum(totals)
    as_float = lambda array: array.astype(jnp.float32)
    enc_params = (as_float(enc_gain1), as_float(enc_bias1), as_float(enc_qkv), as_float(enc_proj), as_float(enc_gain2), as_float(enc_bias2), as_float(enc_fc1), as_float(enc_fc2))
    dec_params = (as_float(dec_gain1), as_float(dec_bias1), as_float(dec_qkv), as_float(dec_proj), as_float(dec_gain2), as_float(dec_bias2), as_float(dec_fc1), as_float(dec_fc2))
    diff_params = (as_float(diff_in), as_float(diff_time1), as_float(diff_time2), as_float(diff_cond), as_float(diff_ada), as_float(diff_mlp1), as_float(diff_mlp2), as_float(diff_final), as_float(diff_out))
    objective_value, backward = jax.vjp(objective, enc_params, dec_params, as_float(mask_token), diff_params, as_float(tokens))
    grad_enc, grad_dec, grad_mask, grad_diff, grad_tokens = backward(jnp.ones((), jnp.float32))
    loss_mean = objective_value / total
    return (loss_mean, grad_tokens, grad_enc[0], grad_enc[1], grad_enc[2], grad_enc[3], grad_enc[4], grad_enc[5], grad_enc[6], grad_enc[7], grad_dec[0], grad_dec[1], grad_dec[2], grad_dec[3], grad_dec[4], grad_dec[5], grad_dec[6], grad_dec[7], grad_mask, grad_diff[0], grad_diff[1], grad_diff[2], grad_diff[3], grad_diff[4], grad_diff[5], grad_diff[6], grad_diff[7], grad_diff[8])
```

```python
import functools
import math

import jax
import jax.numpy as jnp
from jax import lax
from jax.experimental import pallas as pl
from jax.experimental.pallas import tpu as pltpu
from jax.sharding import PartitionSpec as P

HEAD = 64
CH = 16
BUF = 64
L = 256


def split_masks(devices):
    bits = devices.bit_length() - 2
    upper = min(2, bits - 2)
    first = (bits - upper) // 2
    second = bits - upper - first
    group = lambda low, count: [m << low for m in range(1 << count)]
    return group(1, first), group(1 + first, second), group(1 + first + second, upper)


def swap(block, mask, devices):
    return lax.ppermute(block, "dp", [(i, i ^ mask) for i in range(devices)])


def wide(part):
    return part.astype(jnp.float32)


def narrow(part):
    return part.astype(jnp.bfloat16)


def place_kernel(layout, kinds, *refs):
    pieces = refs[: len(layout)]
    outs = refs[len(layout) : len(layout) + len(kinds)]
    sems = refs[-1]
    me = lax.axis_index("dp")
    unit = pieces[0].shape[-1]
    copies = []
    for piece, masks in zip(pieces, layout):
        for spot, mask in enumerate(masks):
            base = 0
            for out, (count, side) in zip(outs, kinds):
                for j in range(count):
                    target = out.at[me ^ mask, j]
                    if side == "columns":
                        target = out.at[me ^ mask, :, pl.ds(j * unit, unit)]
                    copies.append(
                        pltpu.make_async_copy(piece.at[spot, base + j], target, sems.at[len(copies)])
                    )
                base += count
    for copy in copies:
        copy.start()
    for copy in copies:
        copy.wait()


def whole_shape(kind, rows, unit):
    count, side = kind
    return (rows, count * unit) if side == "columns" else (count, rows, unit)


def place(pieces, layout, kinds, devices):
    _, units, rows, unit = pieces[0].shape
    dtype = pieces[0].dtype
    moved = 2 * devices * units * rows * unit * dtype.itemsize
    return pl.pallas_call(
        functools.partial(place_kernel, layout, kinds),
        out_shape=[jax.ShapeDtypeStruct((devices,) + whole_shape(kind, rows, unit), dtype) for kind in kinds],
        in_specs=[pl.BlockSpec(memory_space=pl.ANY)] * len(pieces),
        out_specs=[pl.BlockSpec(memory_space=pltpu.VMEM)] * len(kinds),
        scratch_shapes=[pltpu.SemaphoreType.DMA((devices * units,))],
        compiler_params=pltpu.CompilerParams(vmem_limit_bytes=24 << 20),
        cost_estimate=pl.CostEstimate(flops=0, bytes_accessed=moved, transcendentals=0),
    )(*pieces)


def pin(*trees):
    return lax.optimization_barrier(trees)


class Gather:
    def __init__(self, own, kinds, devices):
        self.kinds, self.devices = kinds, devices
        self.first, self.second, self.upper = split_masks(devices)
        self.state = [own]

    def along_upper(self):
        own = self.state[0]
        self.state = [own] + [swap(own, m, self.devices) for m in self.upper[1:]]

    def near(self):
        half = len(self.upper) // 2
        self.layout, held, self.state = [], self.state, []
        for part, masks in ((0, self.first), (1, self.second)):
            base = self.upper[part * half : (part + 1) * half]
            block = jnp.stack(held[part * half : (part + 1) * half])
            for m in masks:
                self.state.append(block if m == 0 else swap(block, m, self.devices))
                self.layout.append([m ^ v for v in base])

    def far(self):
        held = list(zip(self.state, self.layout))
        cut = len(self.first)
        for group, masks in ((held[:cut], self.second), (held[cut:], self.first)):
            for m in masks[1:]:
                for block, base in group:
                    self.state.append(swap(block, m, self.devices))
                    self.layout.append([m ^ v for v in base])

    def across(self):
        self.state = self.state + [swap(block, 1, self.devices) for block in self.state]
        self.layout = self.layout + [[1 ^ v for v in base] for base in self.layout]

    def whole(self):
        return place(self.state, self.layout, self.kinds, self.devices)


def as_units(shard, unit):
    rows, width = shard.shape
    return shard.reshape(rows, width // unit, unit).transpose(1, 0, 2)


def fold_kernel(sizes, kinds, table, *refs):
    count = len(kinds)
    mine, theirs, outs = refs[:count], refs[count : 2 * count], refs[2 * count :]
    step = pl.program_id(0)
    start = 0
    for out, size in zip(outs, sizes):
        unit = out.shape[-1]

        @pl.when((step >= start) & (step < start + size))
        def _(out=out, unit=unit):
            base = 0
            for own, other, (units, side) in zip(mine, theirs, kinds):
                for j in range(units):
                    spot = (0, j) if side == "rows" else (0, slice(None), slice(j * unit, (j + 1) * unit))
                    out[0, base + j] = narrow(wide(own[spot]) + wide(other[spot]))
                base += units

        start += size


def fold(mine, theirs, kinds, slots, devices):
    unit = theirs[0].shape[-1] // (kinds[0][0] if kinds[0][1] == "columns" else 1)
    rows = theirs[0].shape[-2]
    units = sum(count for count, _ in kinds)
    sizes = [len(group) for group in slots]
    me = lax.axis_index("dp")
    order = jnp.asarray([chip for group in slots for chip in group], jnp.int32)
    table = (me // 2) ^ order
    table = jnp.concatenate([table, (me % 2).reshape(1).astype(jnp.int32)])
    total = len(order)
    zeros = lambda array: (0,) * (array.ndim - 1)
    own_spec = lambda a: pl.BlockSpec((1,) + a.shape[1:], lambda s, t, z=zeros(a): (t[s] * 2 + t[total],) + z)
    other_spec = lambda a: pl.BlockSpec((1,) + a.shape[1:], lambda s, t, z=zeros(a): (t[s],) + z)
    out_specs, start = [], 0
    for size in sizes:
        out_specs.append(
            pl.BlockSpec(
                (1, units, rows, unit), lambda s, t, lo=start, top=size - 1: (jnp.clip(s - lo, 0, top), 0, 0, 0)
            )
        )
        start += size
    moved = 3 * total * units * rows * unit * 2
    return pl.pallas_call(
        functools.partial(fold_kernel, sizes, kinds),
        out_shape=[jax.ShapeDtypeStruct((size, units, rows, unit), jnp.bfloat16) for size in sizes],
        grid_spec=pltpu.PrefetchScalarGridSpec(
            num_scalar_prefetch=1,
            grid=(total,),
            in_specs=[own_spec(a) for a in mine] + [other_spec(a) for a in theirs],
            out_specs=out_specs,
        ),
        compiler_params=pltpu.CompilerParams(
            dimension_semantics=("arbitrary",), vmem_limit_bytes=32 << 20
        ),
        cost_estimate=pl.CostEstimate(flops=moved, bytes_accessed=moved, transcendentals=0),
    )(table, *mine, *theirs)


class Scatter:
    def __init__(self, wholes, kinds, devices):
        self.kinds, self.devices, self.wholes = kinds, devices, wholes
        first, second, upper = ([m // 2 for m in masks] for masks in split_masks(devices))
        half = len(upper) // 2
        self.upper = upper
        self.routes = ((upper[:half], second, first), (upper[half:], first, second))
        core = lax.axis_index("dp") % 2
        self.state = []
        for whole in wholes:
            pairs = whole.reshape((devices // 2, 2) + whole.shape[1:])
            self.state.append(swap(lax.dynamic_index_in_dim(pairs, 1 - core, 1, keepdims=False), 1, devices))

    def near(self):
        slots = [[u ^ n ^ f for f in far for u in ups] for ups, near, far in self.routes for n in near]
        folded = fold(self.wholes, self.state, self.kinds, slots, self.devices)
        self.wholes, self.state, base = None, [], 0
        for _, near, _ in self.routes:
            groups = folded[base : base + len(near)]
            base += len(near)
            self.state += [g if n == 0 else swap(g, 2 * n, self.devices) for g, n in zip(groups, near)]

    def far(self):
        held, self.state = self.state, []
        for ups, near, far in self.routes:
            groups, held = held[: len(near)], held[len(near) :]
            blocks = [wide(g).reshape((len(far), len(ups)) + g.shape[1:]) for g in groups]
            for spot, f in enumerate(far):
                total = blocks[0][spot]
                for block in blocks[1:]:
                    total = total + block[spot]
                total = narrow(total)
                self.state.append(total if f == 0 else swap(total, 2 * f, self.devices))

    def along_upper(self):
        held, parts = self.state, []
        for ups, near, far in self.routes:
            groups, held = held[: len(far)], held[len(far) :]
            for spot in range(len(ups)):
                total = wide(groups[0][spot])
                for g in groups[1:]:
                    total = total + wide(g[spot])
                parts.append(narrow(total))
        self.state = [p if u == 0 else swap(p, 2 * u, self.devices) for p, u in zip(parts, self.upper)]

    def result(self):
        total = wide(self.state[0])
        for part in self.state[1:]:
            total = total + wide(part)
        return total


def from_units(units):
    count, rows, unit = units.shape
    return units.transpose(1, 0, 2).reshape(rows, count * unit)


def scatter_plain(whole, devices):
    first, second, upper = split_masks(devices)
    me = lax.axis_index("dp")
    block = whole
    for masks in (upper, second, first, [0, 1]):
        unit = masks[1]
        count = len(masks)
        spread = block.reshape((count, block.shape[0] // count) + block.shape[1:])
        position = me // unit % count
        total = lax.dynamic_index_in_dim(spread, position, 0, keepdims=False)
        for m in masks[1:]:
            send = lax.dynamic_index_in_dim(spread, position ^ (m // unit), 0, keepdims=False)
            total = total + swap(send, m, devices)
        block = total
    return block[0]


def in_three(values):
    first = lax.reduce_precision(values, 8, 7)
    second = lax.reduce_precision(values - first, 8, 7)
    third = values - first - second
    return [narrow(part) for part in (first, second, third)]


def layer_norm(residual, gain, offset):
    centred = residual - jnp.mean(residual, axis=-1, keepdims=True)
    spread = jnp.mean(centred * centred, axis=-1, keepdims=True)
    return centred * lax.rsqrt(spread + 1e-06) * gain + offset


def plain_norm(residual):
    centred = residual - jnp.mean(residual, axis=-1, keepdims=True)
    spread = jnp.mean(centred * centred, axis=-1, keepdims=True)
    return centred * lax.rsqrt(spread + 1e-06)


def modulate(residual, shift_part, scale_part):
    return plain_norm(residual) * (1.0 + scale_part) + shift_part


def exact_gelu(hidden):
    return jax.nn.gelu(hidden, approximate=False)


def matmul(left, right):
    return jnp.dot(left, right, preferred_element_type=jnp.float32)


def outer_sum(left, right):
    return lax.dot_general(
        left, right, (((0,), (0,)), ((), ())), preferred_element_type=jnp.float32
    )


def times_transpose(left, right):
    return lax.dot_general(
        left, right, (((1,), (1,)), ((), ())), preferred_element_type=jnp.float32
    )


def attention_scores(query_rows, key_rows, keys_live):
    scores = jnp.einsum(
        "bqhe,bkhe->bhqk", query_rows, key_rows, preferred_element_type=jnp.float32
    ) * HEAD ** (-0.5)
    return jnp.where(keys_live[:, None, None, :], scores, -1e30)


def split_heads(projected, images):
    positions = projected.shape[0] // images
    head_count = projected.shape[1] // (3 * HEAD)
    shaped = projected.reshape(images, positions, 3, head_count, HEAD)
    return (shaped[:, :, 0], shaped[:, :, 1], shaped[:, :, 2])


def project_in(residual, gain, offset, qkv_w):
    normed = narrow(layer_norm(residual, wide(gain), wide(offset)))
    return normed, narrow(matmul(normed, qkv_w))


def attend_forward(projected, keys_live, images):
    query_rows, key_rows, value_rows = split_heads(projected, images)
    scores = attention_scores(query_rows, key_rows, keys_live)
    row_peak = jnp.max(scores, axis=-1, keepdims=True)
    log_total = row_peak + jnp.log(jnp.sum(jnp.exp(scores - row_peak), axis=-1, keepdims=True))
    soft_rounded = narrow(jnp.exp(scores - log_total))
    attended = jnp.einsum("bhqk,bkhe->bqhe", soft_rounded, value_rows, preferred_element_type=jnp.float32)
    return log_total, narrow(attended).reshape(projected.shape[0], -1)


def feed_in(residual, attended, proj_w, gain, offset, fc1_w):
    middle = residual + matmul(attended, proj_w)
    normed = narrow(layer_norm(middle, wide(gain), wide(offset)))
    hidden = matmul(normed, fc1_w)
    return middle, normed, hidden, narrow(exact_gelu(hidden))


def feed_backward(grad_output, saved, fc2_w):
    _, normed, hidden, active = saved
    grad_branch = narrow(grad_output)
    grad_active = times_transpose(grad_branch, fc2_w)
    grad_hidden = narrow(jax.vjp(exact_gelu, hidden)[1](grad_active)[0])
    return grad_hidden, narrow(outer_sum(normed, grad_hidden)), narrow(outer_sum(active, grad_branch))


def middle_backward(grad_output, grad_hidden, saved, attended, gain, offset, fc1_w, proj_w):
    grad_normed = times_transpose(grad_hidden, fc1_w)
    back = jax.vjp(layer_norm, saved[0], wide(gain), wide(offset))[1]
    grad_norm, grad_gain, grad_offset = back(grad_normed)
    grad_middle = grad_output + grad_norm
    grad_attention = narrow(grad_middle)
    grad_proj = narrow(outer_sum(attended, grad_attention))
    grad_attended = narrow(times_transpose(grad_attention, proj_w))
    return grad_middle, grad_attended, grad_proj, grad_gain, grad_offset


def attend_backward(grad_attended, projected, log_total, keys_live, images):
    rows, model_width = grad_attended.shape
    grad_attended = grad_attended.reshape(images, rows // images, model_width // HEAD, HEAD)
    query_rows, key_rows, value_rows = split_heads(projected, images)
    scores = attention_scores(query_rows, key_rows, keys_live)
    soft_full = jnp.exp(scores - log_total)
    soft_rounded = narrow(soft_full)
    grad_value = jnp.einsum("bhqk,bqhe->bkhe", soft_rounded, grad_attended, preferred_element_type=jnp.float32)
    grad_soft = jnp.einsum("bqhe,bkhe->bhqk", grad_attended, value_rows, preferred_element_type=jnp.float32)
    grad_scores = soft_full * (grad_soft - jnp.sum(grad_soft * soft_full, axis=-1, keepdims=True))
    grad_scores = narrow(grad_scores)
    grad_query = jnp.einsum(
        "bhqk,bkhe->bqhe", grad_scores, key_rows, preferred_element_type=jnp.float32
    ) * HEAD ** (-0.5)
    grad_key = jnp.einsum(
        "bhqk,bqhe->bkhe", grad_scores, query_rows, preferred_element_type=jnp.float32
    ) * HEAD ** (-0.5)
    grad_projected = narrow(jnp.stack([grad_query, grad_key, grad_value], axis=2))
    return grad_projected.reshape(rows, 3 * model_width)


def inner_backward(grad_middle, grad_projected, residual, gain, offset, qkv_w):
    grad_normed = times_transpose(grad_projected, qkv_w)
    back = jax.vjp(layer_norm, residual, wide(gain), wide(offset))[1]
    grad_norm, grad_gain, grad_offset = back(grad_normed)
    return grad_middle + grad_norm, grad_gain, grad_offset


def diffusion_pass(weights, cond_rows, target_rows, live_flat, step_rows, noise_rows):
    in_w, time1_w, time2_w, cond_w, ada_w, mlp1_w, mlp2_w, final_w, out_w = weights
    copies = step_rows.shape[0]
    count_rows = step_rows.shape[1]
    flat_rows = count_rows * copies
    inner_width = in_w.shape[1]
    steps_float = step_rows.astype(jnp.float32)
    angle_noise = (steps_float / 1000.0 + 0.008) / 1.008 * (math.pi / 2)
    keep_part = jnp.cos(angle_noise) ** 2
    noisy_rows = (
        jnp.sqrt(keep_part)[:, :, None] * target_rows[None, :, :]
        + jnp.sqrt(1.0 - keep_part)[:, :, None] * noise_rows
    )
    noisy_rows = noisy_rows.reshape(flat_rows, CH).astype(jnp.bfloat16)
    start_rows = matmul(noisy_rows, in_w)
    half_freq = time1_w.shape[0] // 2
    frequency = jnp.exp(-math.log(10000.0) * jnp.arange(half_freq, dtype=jnp.float32) / half_freq)
    phases = steps_float.reshape(flat_rows, 1) * frequency[None, :]
    sinusoid = jnp.concatenate([jnp.cos(phases), jnp.sin(phases)], axis=1).astype(jnp.bfloat16)
    time_pre = matmul(sinusoid, time1_w)
    time_active = jax.nn.silu(time_pre).astype(jnp.bfloat16)
    time_emb = matmul(time_active, time2_w)
    cond_emb = matmul(cond_rows, cond_w)
    context_pre = time_emb.reshape(copies, count_rows, inner_width) + cond_emb[None, :, :]
    context = jax.nn.silu(context_pre).astype(jnp.bfloat16).reshape(flat_rows, inner_width)
    modulation = matmul(context, ada_w)
    shift_first = modulation[:, :inner_width]
    scale_first = modulation[:, inner_width : 2 * inner_width]
    gate_first = modulation[:, 2 * inner_width :]
    first_in = modulate(start_rows, shift_first, scale_first).astype(jnp.bfloat16)
    first_pre = matmul(first_in, mlp1_w)
    first_active = jax.nn.silu(first_pre).astype(jnp.bfloat16)
    branch = matmul(first_active, mlp2_w)
    middle = start_rows + gate_first * branch
    final_mod = matmul(context, final_w)
    final_in = modulate(middle, final_mod[:, :inner_width], final_mod[:, inner_width:]).astype(
        jnp.bfloat16
    )
    output = matmul(final_in, out_w)
    residue = output - noise_rows.reshape(flat_rows, CH)
    weight_rows = jnp.tile(live_flat, copies)[:, None]
    partial_sum = jnp.sum(weight_rows * residue * residue) / (copies * CH)
    grad_output = (2.0 * weight_rows * residue / (copies * CH)).astype(jnp.bfloat16)
    grad_out_w = outer_sum(final_in, grad_output)
    grad_final_in = times_transpose(grad_output, out_w)
    final_back = jax.vjp(modulate, middle, final_mod[:, :inner_width], final_mod[:, inner_width:])[
        1
    ]
    grad_middle, grad_shift_final, grad_scale_final = final_back(grad_final_in)
    grad_final_mod = jnp.concatenate([grad_shift_final, grad_scale_final], axis=1).astype(
        jnp.bfloat16
    )
    grad_final_w = outer_sum(context, grad_final_mod)
    grad_context = times_transpose(grad_final_mod, final_w)
    grad_branch = (gate_first * grad_middle).astype(jnp.bfloat16)
    grad_gate = branch * grad_middle
    grad_mlp2 = outer_sum(first_active, grad_branch)
    grad_first_active = times_transpose(grad_branch, mlp2_w)
    silu_back_first = jax.vjp(jax.nn.silu, first_pre)[1]
    grad_first_pre = silu_back_first(grad_first_active)[0].astype(jnp.bfloat16)
    grad_mlp1 = outer_sum(first_in, grad_first_pre)
    grad_first_in = times_transpose(grad_first_pre, mlp1_w)
    first_back = jax.vjp(modulate, start_rows, shift_first, scale_first)[1]
    grad_start_norm, grad_shift_first, grad_scale_first = first_back(grad_first_in)
    grad_modulation = jnp.concatenate(
        [grad_shift_first, grad_scale_first, grad_gate], axis=1
    ).astype(jnp.bfloat16)
    grad_ada = outer_sum(context, grad_modulation)
    grad_context = grad_context + times_transpose(grad_modulation, ada_w)
    silu_back_context = jax.vjp(jax.nn.silu, context_pre)[1]
    grad_context_pre = silu_back_context(grad_context.reshape(copies, count_rows, inner_width))[0]
    grad_time_emb = grad_context_pre.reshape(flat_rows, inner_width).astype(jnp.bfloat16)
    grad_time2 = outer_sum(time_active, grad_time_emb)
    grad_time_active = times_transpose(grad_time_emb, time2_w)
    silu_back_time = jax.vjp(jax.nn.silu, time_pre)[1]
    grad_time_pre = silu_back_time(grad_time_active)[0].astype(jnp.bfloat16)
    grad_time1 = outer_sum(sinusoid, grad_time_pre)
    grad_cond_emb = jnp.sum(grad_context_pre, axis=0).astype(jnp.bfloat16)
    grad_cond_w = outer_sum(cond_rows, grad_cond_emb)
    grad_cond = times_transpose(grad_cond_emb, cond_w).astype(jnp.bfloat16)
    grad_start = (grad_middle + grad_start_norm).astype(jnp.bfloat16)
    grad_in_w = outer_sum(noisy_rows, grad_start)
    grads = (
        grad_in_w,
        grad_time1,
        grad_time2,
        grad_cond_w,
        grad_ada,
        grad_mlp1,
        grad_mlp2,
        grad_final_w,
        grad_out_w,
    )
    return (partial_sum, grad_cond, grads)


def on_device(
    tokens,
    latents,
    orders,
    counts,
    timesteps,
    noise,
    enc_gain1,
    enc_bias1,
    enc_qkv,
    enc_proj,
    enc_gain2,
    enc_bias2,
    enc_fc1,
    enc_fc2,
    dec_gain1,
    dec_bias1,
    dec_qkv,
    dec_proj,
    dec_gain2,
    dec_bias2,
    dec_fc1,
    dec_fc2,
    mask_token,
    diff_in,
    diff_time1,
    diff_time2,
    diff_cond,
    diff_ada,
    diff_mlp1,
    diff_mlp2,
    diff_final,
    diff_out,
):
    devices = lax.axis_size("dp")
    images = tokens.shape[0]
    positions = tokens.shape[1]
    model_width = tokens.shape[2]
    tokens_here = images * L
    shard_rows = enc_proj.shape[0]
    flat_latents = latents.reshape(tokens_here, CH)
    sums_here = jnp.sum(flat_latents, axis=0)
    squares_here = jnp.sum(flat_latents * flat_latents, axis=0)
    count_here = jnp.sum(counts).astype(jnp.float32)
    statistics = jnp.concatenate([sums_here, squares_here, count_here[None]])
    vectors = [enc_gain1, enc_bias1, enc_gain2, enc_bias2, dec_gain1, dec_bias1, dec_gain2, dec_bias2, mask_token]
    statistics = jnp.concatenate(in_three(statistics))[None]
    packed = jnp.concatenate(
        [
            jnp.pad(jnp.stack(vectors, axis=1), ((0, 0), (0, 128 - len(vectors)))),
            jnp.pad(statistics, ((0, shard_rows - 1), (0, model_width - 128 - statistics.shape[1]))),
        ],
        axis=1,
    )[None]

    inner_width = diff_mlp1.shape[1]
    final_shard = jnp.concatenate([diff_ada, diff_final], axis=1)
    enc_shard = jnp.concatenate([enc_fc1] + list(enc_fc2.reshape(-1, shard_rows, model_width)), axis=1)
    ends = jnp.pad(jnp.concatenate([diff_in.T, diff_out], axis=1), ((0, 0), (0, inner_width - 2 * CH)))
    diff_units = jnp.stack([diff_time2, diff_mlp1, diff_mlp2, jnp.concatenate([diff_cond, diff_time1], axis=0), ends])

    qkv_kinds, proj_kinds = ((3, "columns"),), ((1, "columns"),)
    fc_count = enc_fc1.shape[1] // model_width
    late_kinds = proj_kinds + ((fc_count, "columns"), (fc_count, "rows"))

    def early_units(qkv, proj, extra):
        return jnp.concatenate([as_units(qkv, model_width), proj[None]] + extra, axis=0)

    def late_units(fc1, fc2):
        return jnp.concatenate([as_units(fc1, model_width), fc2.reshape(-1, shard_rows, model_width)], axis=0)

    enc_early = Gather(early_units(enc_qkv, enc_proj, [packed]), qkv_kinds + proj_kinds + proj_kinds, devices)
    dec_early = Gather(early_units(dec_qkv, dec_proj, []), qkv_kinds + proj_kinds, devices)
    dec_late = Gather(late_units(dec_fc1, dec_fc2), late_kinds[1:], devices)
    diff_rest = Gather(diff_units, ((1, "columns"),) * 5, devices)

    enc_wide = lax.all_gather(enc_shard, "dp", axis=0, tiled=True)
    final_wide = lax.all_gather(final_shard, "dp", axis=0, tiled=True)
    enc_early.along_upper()
    enc_early.state, dec_early.state = pin(enc_early.state, dec_early.state)
    enc_early.near()
    dec_early.along_upper()
    (enc_early.state,) = pin(enc_early.state)
    enc_early.far()
    enc_early.state, dec_early.state, dec_late.state = pin(enc_early.state, dec_early.state, dec_late.state)
    enc_early.across()
    dec_early.near()
    dec_late.along_upper()
    enc_early.state, dec_early.state = pin(enc_early.state, dec_early.state)
    dec_early.far()
    enc_qkv_whole, enc_proj_whole, small_full = enc_early.whole()
    enc_qkv_whole, enc_proj_whole = (part.reshape(model_width, -1) for part in (enc_qkv_whole, enc_proj_whole))

    vectors = list(wide(small_full.reshape(model_width, -1)[:, :16].T))
    statistics = wide(small_full.reshape(devices, shard_rows, -1)[:, 0, 128 : 128 + 3 * (2 * CH + 1)])
    statistics = jnp.sum(jnp.sum(statistics.reshape(devices, 3, -1), axis=1), axis=0)
    sums_all, squares_all, count_all = statistics[:CH], statistics[CH : 2 * CH], statistics[2 * CH]
    cell_count = tokens_here * devices
    average = sums_all / cell_count
    spread = squares_all / cell_count - average * average
    target = ((flat_latents - average) * lax.rsqrt(spread + 1e-06)).astype(jnp.bfloat16)

    masked = (orders < counts[:, None]).astype(jnp.int32)
    flag_rows = masked.reshape(tokens_here)
    rank_rows = jnp.cumsum(flag_rows) - flag_rows
    slot_count = -(-tokens_here // devices)
    copies = timesteps.shape[1]
    drawn = jnp.concatenate(
        [noise.reshape(devices, slot_count, -1), timesteps.astype(jnp.float32).reshape(devices, slot_count, -1)], axis=2
    )
    drawn = lax.all_to_all(drawn, "dp", split_axis=0, concat_axis=0, tiled=True)
    drawn = drawn.reshape(devices * slot_count, -1)
    slots = jnp.arange(devices * slot_count, dtype=jnp.int32)
    ranks = slots % slot_count * devices + slots // slot_count
    chooser = (ranks[None, :] == rank_rows[:, None]) & (flag_rows[:, None] > 0)
    drawn = jnp.dot(
        chooser.astype(jnp.float32), drawn, precision=lax.Precision.HIGHEST, preferred_element_type=jnp.float32
    )
    noise_rows = drawn[:, : copies * CH].reshape(tokens_here, copies, CH).transpose(1, 0, 2)
    step_rows = drawn[:, copies * CH :].T

    mask_vector = vectors[8].astype(jnp.float32)

    live_keys = jnp.concatenate([jnp.ones((images, BUF), jnp.int32), 1 - masked], axis=1) > 0
    all_live = jnp.ones((images, positions), jnp.bool_)
    live_rows = live_keys.reshape(images * positions, 1)
    residual = tokens.astype(jnp.float32).reshape(images * positions, model_width)
    enc_normed, enc_projected = project_in(residual, vectors[0], vectors[1], enc_qkv_whole)
    enc_projected, dec_early.state, dec_late.state, diff_rest.state = pin(
        enc_projected, dec_early.state, dec_late.state, diff_rest.state
    )
    dec_early.across()
    dec_late.near()
    diff_rest.along_upper()
    enc_log, enc_attended = attend_forward(enc_projected, live_keys, images)
    enc_attended, dec_early.state, dec_late.state = pin(enc_attended, dec_early.state, dec_late.state)
    dec_late.far()
    dec_qkv_whole, dec_proj_whole = (whole.reshape(model_width, -1) for whole in dec_early.whole())
    enc_fc1_whole = enc_wide[:, : fc_count * model_width]
    enc_fc2_whole = [
        enc_wide[:, (fc_count + i) * model_width : (fc_count + i + 1) * model_width] for i in range(fc_count)
    ]
    enc_fc2_whole = jnp.stack([part.reshape(devices, shard_rows, -1) for part in enc_fc2_whole], axis=1)
    enc_fc2_whole = enc_fc2_whole.reshape(-1, model_width)
    enc_feed = feed_in(residual, enc_attended, enc_proj_whole, vectors[2], vectors[3], enc_fc1_whole)
    enc_feed, dec_late.state, diff_rest.state = pin(enc_feed, dec_late.state, diff_rest.state)
    dec_late.across()
    diff_rest.near()
    encoded = enc_feed[0] + matmul(enc_feed[3], enc_fc2_whole)
    decoder_in = jnp.where(live_rows, encoded, mask_vector[None, :])
    dec_normed, dec_projected = project_in(decoder_in, vectors[4], vectors[5], dec_qkv_whole)
    dec_projected, dec_late.state, diff_rest.state = pin(dec_projected, dec_late.state, diff_rest.state)
    diff_rest.far()
    dec_fc1_whole, dec_fc2_whole = (whole.reshape(-1, whole.shape[-1]) for whole in dec_late.whole())
    dec_log, dec_attended = attend_forward(dec_projected, all_live, images)
    dec_feed = feed_in(decoder_in, dec_attended, dec_proj_whole, vectors[6], vectors[7], dec_fc1_whole)
    dec_feed, diff_rest.state = pin(dec_feed, diff_rest.state)
    diff_rest.across()
    decoded = dec_feed[0] + matmul(dec_feed[3], dec_fc2_whole)
    time2_full, mlp1_full, mlp2_full, mixed, ends = (whole.reshape(-1, inner_width) for whole in diff_rest.whole())
    in_full, out_full = ends[:, :CH].T, ends[:, CH : 2 * CH]
    mixed = mixed.reshape(devices, -1, inner_width)
    cond_full = mixed[:, :shard_rows].reshape(-1, inner_width)
    time1_full = mixed[:, shard_rows:].reshape(-1, inner_width)
    ada_full, final_full = final_wide[:, : 3 * inner_width], final_wide[:, 3 * inner_width :]
    diff_full = (in_full, time1_full, time2_full, cond_full, ada_full, mlp1_full, mlp2_full, final_full, out_full)
    cond_here = decoded.reshape(images, positions, model_width)[:, BUF:]
    cond_here = cond_here.reshape(tokens_here, model_width).astype(jnp.bfloat16)
    partial_sum, grad_cond, diff_grads = diffusion_pass(
        diff_full, cond_here, target.astype(jnp.float32), flag_rows.astype(jnp.float32), step_rows, noise_rows
    )
    by_device = lambda part: narrow(part).reshape(devices, -1, part.shape[1])
    mixed = jnp.concatenate([by_device(diff_grads[3]), by_device(diff_grads[1])], axis=1).reshape(-1, inner_width)
    diff_sum = [narrow(diff_grads[i]) for i in (2, 5, 6, 4, 7)] + [mixed]
    grad_cond, diff_sum = pin(grad_cond, jnp.concatenate(diff_sum, axis=1))
    diff_sum = lax.psum_scatter(diff_sum, "dp", scatter_dimension=0, tiled=True)
    columns_sum = lambda lo, hi: wide(diff_sum[:, lo * inner_width : hi * inner_width])
    mixed = columns_sum(8, 9)

    def scatter_late(fc1, fc2):
        fc1, fc2 = by_device(fc1), fc2.reshape(devices, -1, shard_rows, model_width)
        return Scatter([fc1, fc2], late_kinds[1:], devices)

    def scatter_early(qkv, proj):
        return Scatter([by_device(qkv), by_device(proj)], qkv_kinds + proj_kinds, devices)

    grad_decoded = jnp.concatenate(
        [
            jnp.zeros((images, BUF, model_width), jnp.float32),
            grad_cond.astype(jnp.float32).reshape(images, L, model_width),
        ],
        axis=1,
    )
    grad_decoded = grad_decoded.reshape(images * positions, model_width)
    grad_hidden, grad_fc1, grad_fc2 = feed_backward(grad_decoded, dec_feed, dec_fc2_whole)
    grad_hidden, grad_fc1, grad_fc2 = pin(grad_hidden, grad_fc1, grad_fc2)
    dec_late = scatter_late(grad_fc1, grad_fc2)
    grad_middle, grad_attended, grad_proj, dec_gain2_grad, dec_bias2_grad = middle_backward(
        grad_decoded, grad_hidden, dec_feed, dec_attended, vectors[6], vectors[7], dec_fc1_whole, dec_proj_whole
    )
    grad_attended, dec_late.state = pin(grad_attended, dec_late.state)
    dec_late.near()
    grad_projected = attend_backward(grad_attended, dec_projected, dec_log, all_live, images)
    grad_qkv = narrow(outer_sum(dec_normed, grad_projected))
    dec_early = scatter_early(grad_qkv, grad_proj)
    grad_decoder_in, dec_gain1_grad, dec_bias1_grad = inner_backward(
        grad_middle, grad_projected, decoder_in, vectors[4], vectors[5], dec_qkv_whole
    )
    grad_mask = jnp.sum(jnp.where(live_rows, 0.0, grad_decoder_in), axis=0)
    grad_encoded = jnp.where(live_rows, grad_decoder_in, 0.0)
    grad_encoded, dec_late.state, dec_early.state = pin(grad_encoded, dec_late.state, dec_early.state)
    dec_late.far()
    dec_early.near()

    grad_hidden, grad_fc1, grad_fc2 = feed_backward(grad_encoded, enc_feed, enc_fc2_whole)
    grad_hidden, grad_fc1, grad_fc2, dec_late.state, dec_early.state = pin(
        grad_hidden, grad_fc1, grad_fc2, dec_late.state, dec_early.state
    )
    dec_late.along_upper()
    enc_late = scatter_late(grad_fc1, grad_fc2)
    grad_middle, grad_attended, grad_proj, enc_gain2_grad, enc_bias2_grad = middle_backward(
        grad_encoded, grad_hidden, enc_feed, enc_attended, vectors[2], vectors[3], enc_fc1_whole, enc_proj_whole
    )
    grad_attended, enc_late.state, dec_early.state = pin(grad_attended, enc_late.state, dec_early.state)
    dec_early.far()
    enc_late.near()
    grad_projected = attend_backward(grad_attended, enc_projected, enc_log, live_keys, images)
    grad_qkv = narrow(outer_sum(enc_normed, grad_projected))
    grad_projected, grad_qkv, enc_late.state, dec_early.state = pin(
        grad_projected, grad_qkv, enc_late.state, dec_early.state
    )
    enc_early = scatter_early(grad_qkv, grad_proj)
    enc_late.far()
    dec_early.along_upper()
    grad_residual, enc_gain1_grad, enc_bias1_grad = inner_backward(
        grad_middle, grad_projected, residual, vectors[0], vectors[1], enc_qkv_whole
    )
    grad_residual, enc_late.state, enc_early.state = pin(grad_residual, enc_late.state, enc_early.state)
    enc_late.along_upper()
    enc_early.near()
    enc_late.state, enc_early.state = pin(enc_late.state, enc_early.state)
    enc_early.far()
    (enc_early.state,) = pin(enc_early.state)
    enc_early.along_upper()

    def block_sums(early, late):
        early, late = early.result(), late.result()
        return [from_units(early[:3]), early[3], from_units(late[:fc_count]), late[fc_count:].reshape(-1, model_width)]

    dec_big = block_sums(dec_early, dec_late)
    enc_big = block_sums(enc_early, enc_late)
    grad_small = [enc_gain1_grad, enc_bias1_grad, enc_gain2_grad, enc_bias2_grad]
    grad_small += [dec_gain1_grad, dec_bias1_grad, dec_gain2_grad, dec_bias2_grad, grad_mask]
    grad_small = jnp.stack(grad_small + [jnp.full((model_width,), partial_sum, jnp.float32)])
    small_count = grad_small.shape[0]
    packed = grad_small.reshape(small_count, devices, -1).transpose(1, 0, 2).reshape(devices, -1)
    ends = jnp.concatenate([diff_grads[0].T, diff_grads[8]], axis=1).reshape(devices, -1)
    packed = jnp.concatenate([packed, ends], axis=1)
    packed = jnp.pad(packed, ((0, 0), (0, -packed.shape[1] % 128))).reshape(devices, -1, 128)
    summed = scatter_plain(packed, devices).reshape(-1)
    ends = summed[small_count * shard_rows :][: ends.shape[1]].reshape(-1, 2 * CH)
    summed = summed[: small_count * shard_rows].reshape(small_count, -1)
    enc_summed = (summed[0], summed[1], enc_big[0], enc_big[1], summed[2], summed[3], enc_big[2], enc_big[3])
    dec_summed = (summed[4], summed[5], dec_big[0], dec_big[1], summed[6], summed[7], dec_big[2], dec_big[3], summed[8])
    diff_summed = (
        ends[:, :CH].T,
        mixed[shard_rows:],
        columns_sum(0, 1),
        mixed[:shard_rows],
        columns_sum(3, 6),
        columns_sum(1, 2),
        columns_sum(2, 3),
        columns_sum(6, 8),
        ends[:, CH:],
    )
    loss_mean = summed[9][0] / count_all
    grad_tokens = grad_residual.reshape(images, positions, model_width)
    return (
        loss_mean,
        grad_tokens,
        enc_summed[0],
        enc_summed[1],
        enc_summed[2],
        enc_summed[3],
        enc_summed[4],
        enc_summed[5],
        enc_summed[6],
        enc_summed[7],
        dec_summed[0],
        dec_summed[1],
        dec_summed[2],
        dec_summed[3],
        dec_summed[4],
        dec_summed[5],
        dec_summed[6],
        dec_summed[7],
        dec_summed[8],
        diff_summed[0],
        diff_summed[1],
        diff_summed[2],
        diff_summed[3],
        diff_summed[4],
        diff_summed[5],
        diff_summed[6],
        diff_summed[7],
        diff_summed[8],
    )


def solution(mesh):
    placed = (
        P("dp", None, None),
        P("dp", None, None),
        P("dp", None),
        P("dp"),
        P("dp", None),
        P("dp", None, None),
        P("dp"),
        P("dp"),
        P("dp", None),
        P("dp", None),
        P("dp"),
        P("dp"),
        P("dp", None),
        P("dp", None),
        P("dp"),
        P("dp"),
        P("dp", None),
        P("dp", None),
        P("dp"),
        P("dp"),
        P("dp", None),
        P("dp", None),
        P("dp"),
        P(None, "dp"),
        P("dp", None),
        P("dp", None),
        P("dp", None),
        P("dp", None),
        P("dp", None),
        P("dp", None),
        P("dp", None),
        P("dp", None),
    )
    return jax.shard_map(
        on_device,
        mesh=mesh,
        in_specs=placed,
        out_specs=(
            P(),
            P("dp", None, None),
            P("dp"),
            P("dp"),
            P("dp", None),
            P("dp", None),
            P("dp"),
            P("dp"),
            P("dp", None),
            P("dp", None),
            P("dp"),
            P("dp"),
            P("dp", None),
            P("dp", None),
            P("dp"),
            P("dp"),
            P("dp", None),
            P("dp", None),
            P("dp"),
            P(None, "dp"),
            P("dp", None),
            P("dp", None),
            P("dp", None),
            P("dp", None),
            P("dp", None),
            P("dp", None),
            P("dp", None),
            P("dp", None),
        ),
        check_vma=False,
    )
```

```python
import functools
import math

import jax
import jax.numpy as jnp
from jax import lax
from jax.experimental import pallas as pl
from jax.experimental.pallas import tpu as pltpu
from jax.sharding import PartitionSpec as P

HEAD = 64
CH = 16
BUF = 64
L = 256


def split_masks(devices):
    bits = devices.bit_length() - 2
    upper = min(2, bits - 2)
    first = (bits - upper) // 2
    second = bits - upper - first
    group = lambda low, count: [m << low for m in range(1 << count)]
    return group(1, first), group(1 + first, second), group(1 + first + second, upper)


def swap(block, mask, devices):
    return lax.ppermute(block, "dp", [(i, i ^ mask) for i in range(devices)])


def wide(part):
    return part.astype(jnp.float32)


def narrow(part):
    return part.astype(jnp.bfloat16)


def place_kernel(layout, kinds, *refs):
    pieces = refs[: len(layout)]
    outs = refs[len(layout) : len(layout) + len(kinds)]
    sems = refs[-1]
    me = lax.axis_index("dp")
    unit = pieces[0].shape[-1]
    copies = []
    for piece, masks in zip(pieces, layout):
        for spot, mask in enumerate(masks):
            base = 0
            for out, (count, side) in zip(outs, kinds):
                for j in range(count):
                    target = out.at[me ^ mask, j]
                    if side == "columns":
                        target = out.at[me ^ mask, :, pl.ds(j * unit, unit)]
                    copies.append(
                        pltpu.make_async_copy(piece.at[spot, base + j], target, sems.at[len(copies)])
                    )
                base += count
    for copy in copies:
        copy.start()
    for copy in copies:
        copy.wait()


def whole_shape(kind, rows, unit):
    count, side = kind
    return (rows, count * unit) if side == "columns" else (count, rows, unit)


def place(pieces, layout, kinds, devices):
    _, units, rows, unit = pieces[0].shape
    dtype = pieces[0].dtype
    moved = 2 * devices * units * rows * unit * dtype.itemsize
    return pl.pallas_call(
        functools.partial(place_kernel, layout, kinds),
        out_shape=[jax.ShapeDtypeStruct((devices,) + whole_shape(kind, rows, unit), dtype) for kind in kinds],
        in_specs=[pl.BlockSpec(memory_space=pl.ANY)] * len(pieces),
        out_specs=[pl.BlockSpec(memory_space=pltpu.VMEM)] * len(kinds),
        scratch_shapes=[pltpu.SemaphoreType.DMA((devices * units,))],
        compiler_params=pltpu.CompilerParams(vmem_limit_bytes=24 << 20),
        cost_estimate=pl.CostEstimate(flops=0, bytes_accessed=moved, transcendentals=0),
    )(*pieces)


def pin(*trees):
    return lax.optimization_barrier(trees)


class Gather:
    def __init__(self, own, kinds, devices):
        self.kinds, self.devices = kinds, devices
        self.first, self.second, self.upper = split_masks(devices)
        self.state = [own]

    def along_upper(self):
        own = self.state[0]
        self.state = [own] + [swap(own, m, self.devices) for m in self.upper[1:]]

    def near(self):
        half = len(self.upper) // 2
        self.layout, held, self.state = [], self.state, []
        for part, masks in ((0, self.first), (1, self.second)):
            base = self.upper[part * half : (part + 1) * half]
            block = jnp.stack(held[part * half : (part + 1) * half])
            self.state.append([block if m == 0 else swap(block, m, self.devices) for m in masks])
            self.layout.append([m ^ v for m in masks for v in base])

    def far(self):
        self.state = [jnp.concatenate(blocks, axis=0) for blocks in self.state]
        for block, base, masks in zip(self.state[:2], self.layout[:2], (self.second, self.first)):
            for m in masks[1:]:
                self.state.append(swap(block, m, self.devices))
                self.layout.append([m ^ v for v in base])
        self.across(0, 2)

    def across(self, start, stop):
        self.state += [swap(block, 1, self.devices) for block in self.state[start:stop]]
        self.layout += [[1 ^ v for v in base] for base in self.layout[start:stop]]

    def last(self):
        self.across(2, len(self.state) - 2)

    def whole(self):
        return place(self.state, self.layout, self.kinds, self.devices)


def as_units(shard, unit):
    rows, width = shard.shape
    return shard.reshape(rows, width // unit, unit).transpose(1, 0, 2)


def fold_kernel(sizes, kinds, table, *refs):
    count = len(kinds)
    mine, theirs, outs = refs[:count], refs[count : 2 * count], refs[2 * count :]
    step = pl.program_id(0)
    start = 0
    for out, size in zip(outs, sizes):
        unit = out.shape[-1]

        @pl.when((step >= start) & (step < start + size))
        def _(out=out, unit=unit):
            base = 0
            for own, other, (units, side) in zip(mine, theirs, kinds):
                for j in range(units):
                    spot = (0, j) if side == "rows" else (0, slice(None), slice(j * unit, (j + 1) * unit))
                    out[0, base + j] = narrow(wide(own[spot]) + wide(other[spot]))
                base += units

        start += size


def fold(mine, theirs, kinds, slots, devices):
    unit = theirs[0].shape[-1] // (kinds[0][0] if kinds[0][1] == "columns" else 1)
    rows = theirs[0].shape[-2]
    units = sum(count for count, _ in kinds)
    sizes = [len(group) for group in slots]
    me = lax.axis_index("dp")
    order = jnp.asarray([chip for group in slots for chip in group], jnp.int32)
    table = (me // 2) ^ order
    table = jnp.concatenate([table, (me % 2).reshape(1).astype(jnp.int32)])
    total = len(order)
    zeros = lambda array: (0,) * (array.ndim - 1)
    own_spec = lambda a: pl.BlockSpec((1,) + a.shape[1:], lambda s, t, z=zeros(a): (t[s] * 2 + t[total],) + z)
    other_spec = lambda a: pl.BlockSpec((1,) + a.shape[1:], lambda s, t, z=zeros(a): (t[s],) + z)
    out_specs, start = [], 0
    for size in sizes:
        out_specs.append(
            pl.BlockSpec(
                (1, units, rows, unit), lambda s, t, lo=start, top=size - 1: (jnp.clip(s - lo, 0, top), 0, 0, 0)
            )
        )
        start += size
    moved = 3 * total * units * rows * unit * 2
    return pl.pallas_call(
        functools.partial(fold_kernel, sizes, kinds),
        out_shape=[jax.ShapeDtypeStruct((size, units, rows, unit), jnp.bfloat16) for size in sizes],
        grid_spec=pltpu.PrefetchScalarGridSpec(
            num_scalar_prefetch=1,
            grid=(total,),
            in_specs=[own_spec(a) for a in mine] + [other_spec(a) for a in theirs],
            out_specs=out_specs,
        ),
        compiler_params=pltpu.CompilerParams(
            dimension_semantics=("arbitrary",), vmem_limit_bytes=32 << 20
        ),
        cost_estimate=pl.CostEstimate(flops=moved, bytes_accessed=moved, transcendentals=0),
    )(table, *mine, *theirs)


class Scatter:
    def __init__(self, wholes, kinds, devices):
        self.kinds, self.devices, self.wholes = kinds, devices, wholes
        first, second, upper = ([m // 2 for m in masks] for masks in split_masks(devices))
        half = len(upper) // 2
        self.upper = upper
        self.routes = ((upper[:half], second, first), (upper[half:], first, second))
        core = lax.axis_index("dp") % 2
        self.state = []
        for whole in wholes:
            pairs = whole.reshape((devices // 2, 2) + whole.shape[1:])
            self.state.append(swap(lax.dynamic_index_in_dim(pairs, 1 - core, 1, keepdims=False), 1, devices))

    def fold(self):
        slots = [[u ^ n ^ f for f in far for u in ups] for ups, near, far in self.routes for n in near]
        self.state = fold(self.wholes, self.state, self.kinds, slots, self.devices)
        self.wholes = None

    def near(self):
        masks = [n for _, near, _ in self.routes for n in near]
        self.state = [g if n == 0 else swap(g, 2 * n, self.devices) for g, n in zip(self.state, masks)]

    def far(self):
        held, self.state = self.state, []
        for ups, near, far in self.routes:
            groups, held = held[: len(near)], held[len(near) :]
            blocks = [wide(g).reshape((len(far), len(ups)) + g.shape[1:]) for g in groups]
            for spot, f in enumerate(far):
                total = blocks[0][spot]
                for block in blocks[1:]:
                    total = total + block[spot]
                total = narrow(total)
                self.state.append(total if f == 0 else swap(total, 2 * f, self.devices))

    def along_upper(self):
        held, parts = self.state, []
        for ups, near, far in self.routes:
            groups, held = held[: len(far)], held[len(far) :]
            for spot in range(len(ups)):
                total = wide(groups[0][spot])
                for g in groups[1:]:
                    total = total + wide(g[spot])
                parts.append(narrow(total))
        self.state = [p if u == 0 else swap(p, 2 * u, self.devices) for p, u in zip(parts, self.upper)]

    def result(self):
        total = wide(self.state[0])
        for part in self.state[1:]:
            total = total + wide(part)
        return total


def from_units(units):
    count, rows, unit = units.shape
    return units.transpose(1, 0, 2).reshape(rows, count * unit)


def sum_all(block, devices):
    mask = 1
    while mask < devices:
        block = block + swap(block, mask, devices)
        mask *= 2
    return block


def in_three(values):
    first = lax.reduce_precision(values, 8, 7)
    second = lax.reduce_precision(values - first, 8, 7)
    third = values - first - second
    return [narrow(part) for part in (first, second, third)]


def layer_norm(residual, gain, offset):
    centred = residual - jnp.mean(residual, axis=-1, keepdims=True)
    spread = jnp.mean(centred * centred, axis=-1, keepdims=True)
    return centred * lax.rsqrt(spread + 1e-06) * gain + offset


def plain_norm(residual):
    centred = residual - jnp.mean(residual, axis=-1, keepdims=True)
    spread = jnp.mean(centred * centred, axis=-1, keepdims=True)
    return centred * lax.rsqrt(spread + 1e-06)


def modulate(residual, shift_part, scale_part):
    return plain_norm(residual) * (1.0 + scale_part) + shift_part


def exact_gelu(hidden):
    below = 0.5 + 0.5 * lax.erf(hidden * math.sqrt(0.5))
    density = jnp.exp(-0.5 * hidden * hidden) * (1.0 / math.sqrt(2.0 * math.pi))
    return hidden * below, below + hidden * density


def matmul(left, right):
    return jnp.dot(left, right, preferred_element_type=jnp.float32)


def outer_sum(left, right):
    return lax.dot_general(
        left, right, (((0,), (0,)), ((), ())), preferred_element_type=jnp.float32
    )


def times_transpose(left, right):
    return lax.dot_general(
        left, right, (((1,), (1,)), ((), ())), preferred_element_type=jnp.float32
    )


def attention_scores(query_rows, key_rows, keys_live):
    scores = jnp.einsum(
        "bqhe,bkhe->bhqk", query_rows, key_rows, preferred_element_type=jnp.float32
    ) * HEAD ** (-0.5)
    return jnp.where(keys_live[:, None, None, :], scores, -1e30)


def split_heads(projected, images):
    positions = projected.shape[0] // images
    head_count = projected.shape[1] // (3 * HEAD)
    shaped = projected.reshape(images, positions, 3, head_count, HEAD)
    return (shaped[:, :, 0], shaped[:, :, 1], shaped[:, :, 2])


def project_in(residual, gain, offset, qkv_w):
    normed = narrow(layer_norm(residual, wide(gain), wide(offset)))
    return normed, narrow(matmul(normed, qkv_w))


def attend_forward(projected, keys_live, images):
    query_rows, key_rows, value_rows = split_heads(projected, images)
    scores = attention_scores(query_rows, key_rows, keys_live)
    row_peak = jnp.max(scores, axis=-1, keepdims=True)
    log_total = row_peak + jnp.log(jnp.sum(jnp.exp(scores - row_peak), axis=-1, keepdims=True))
    soft_rounded = narrow(jnp.exp(scores - log_total))
    attended = jnp.einsum("bhqk,bkhe->bqhe", soft_rounded, value_rows, preferred_element_type=jnp.float32)
    return log_total, narrow(attended).reshape(projected.shape[0], -1)


def feed_in(residual, attended, proj_w, gain, offset, fc1_w):
    middle = residual + matmul(attended, proj_w)
    normed = narrow(layer_norm(middle, wide(gain), wide(offset)))
    active, slope = exact_gelu(matmul(normed, fc1_w))
    return middle, normed, slope, narrow(active)


def feed_backward(grad_output, saved, fc2_w):
    _, normed, slope, active = saved
    grad_branch = narrow(grad_output)
    grad_active = times_transpose(grad_branch, fc2_w)
    grad_hidden = narrow(grad_active * slope)
    return grad_hidden, narrow(outer_sum(normed, grad_hidden)), narrow(outer_sum(active, grad_branch))


def middle_backward(grad_output, grad_hidden, saved, attended, gain, offset, fc1_w, proj_w):
    grad_normed = times_transpose(grad_hidden, fc1_w)
    back = jax.vjp(layer_norm, saved[0], wide(gain), wide(offset))[1]
    grad_norm, grad_gain, grad_offset = back(grad_normed)
    grad_middle = grad_output + grad_norm
    grad_attention = narrow(grad_middle)
    grad_proj = narrow(outer_sum(attended, grad_attention))
    grad_attended = narrow(times_transpose(grad_attention, proj_w))
    return grad_middle, grad_attended, grad_proj, grad_gain, grad_offset


def attend_backward(grad_attended, projected, log_total, keys_live, images):
    rows, model_width = grad_attended.shape
    grad_attended = grad_attended.reshape(images, rows // images, model_width // HEAD, HEAD)
    query_rows, key_rows, value_rows = split_heads(projected, images)
    scores = attention_scores(query_rows, key_rows, keys_live)
    soft_full = jnp.exp(scores - log_total)
    soft_rounded = narrow(soft_full)
    grad_value = jnp.einsum("bhqk,bqhe->bkhe", soft_rounded, grad_attended, preferred_element_type=jnp.float32)
    grad_soft = jnp.einsum("bqhe,bkhe->bhqk", grad_attended, value_rows, preferred_element_type=jnp.float32)
    grad_scores = soft_full * (grad_soft - jnp.sum(grad_soft * soft_full, axis=-1, keepdims=True))
    grad_scores = narrow(grad_scores)
    grad_query = jnp.einsum(
        "bhqk,bkhe->bqhe", grad_scores, key_rows, preferred_element_type=jnp.float32
    ) * HEAD ** (-0.5)
    grad_key = jnp.einsum(
        "bhqk,bqhe->bkhe", grad_scores, query_rows, preferred_element_type=jnp.float32
    ) * HEAD ** (-0.5)
    grad_projected = narrow(jnp.stack([grad_query, grad_key, grad_value], axis=2))
    return grad_projected.reshape(rows, 3 * model_width)


def inner_backward(grad_middle, grad_projected, residual, gain, offset, qkv_w):
    grad_normed = times_transpose(grad_projected, qkv_w)
    back = jax.vjp(layer_norm, residual, wide(gain), wide(offset))[1]
    grad_norm, grad_gain, grad_offset = back(grad_normed)
    return grad_middle + grad_norm, grad_gain, grad_offset


def silu_slope(value):
    gate = jax.nn.sigmoid(value)
    return gate * (1.0 + value * (1.0 - gate))


def normed_rows(value):
    centred = value - jnp.mean(value, axis=-1, keepdims=True)
    inverse = lax.rsqrt(jnp.mean(centred * centred, axis=-1, keepdims=True) + 1e-06)
    return centred * inverse, inverse


def norm_back(grad, normed, inverse):
    spread = jnp.mean(grad * normed, axis=-1, keepdims=True)
    return inverse * (grad - jnp.mean(grad, axis=-1, keepdims=True) - normed * spread)


def head_kernel(
    noisy, noise, sinusoid, live, cond, in_w, time1_w, time2_w, cond_w, wide_w, mlp_w, out_w,
    lefts, rights, grad_time_pre, final_in, grad_output, grad_start, grad_cond_emb, grad_cond, loss,
    time_pre, context_pre, start, first_pre, branch, middle, product, modulation, total,
):
    step = pl.program_id(0)
    rows, width = time_pre.shape
    part = lambda array, i, count=1: array.at[:, i * width : (i + count) * width]

    def by_rows(body):
        size = 32

        def visit(i, carry):
            body(pl.ds(pl.multiple_of(i * size, size), size))
            return carry

        lax.fori_loop(0, rows // size, visit, 0)

    def columns(i):
        return slice(i * width, (i + 1) * width)

    time_pre[...] = matmul(sinusoid[...], time1_w[...])

    def time_rows(r):
        lefts[r, columns(0)] = narrow(jax.nn.silu(time_pre[r, :]))

    by_rows(time_rows)
    context_pre[...] = matmul(part(lefts, 0)[...], time2_w[...]) + matmul(cond[...], cond_w[...])

    def context_rows(r):
        lefts[r, columns(3)] = narrow(jax.nn.silu(context_pre[r, :]))

    by_rows(context_rows)
    for i in range(5):
        part(modulation, i)[...] = matmul(part(lefts, 3)[...], part(wide_w, i)[...])
    start[...] = matmul(noisy[...], in_w[...])

    def first_rows(r):
        normed, _ = normed_rows(start[r, :])
        lefts[r, columns(1)] = narrow(normed * (1.0 + modulation[r, columns(1)]) + modulation[r, columns(0)])

    by_rows(first_rows)
    first_pre[...] = matmul(part(lefts, 1)[...], part(mlp_w, 0)[...])

    def active_rows(r):
        lefts[r, columns(2)] = narrow(jax.nn.silu(first_pre[r, :]))

    by_rows(active_rows)
    branch[...] = matmul(part(lefts, 2)[...], part(mlp_w, 1)[...])

    def middle_rows(r):
        value = start[r, :] + modulation[r, columns(2)] * branch[r, :]
        middle[r, :] = value
        normed, _ = normed_rows(value)
        final_in[r, :] = narrow(normed * (1.0 + modulation[r, columns(4)]) + modulation[r, columns(3)])

    by_rows(middle_rows)
    residue = times_transpose(final_in[...], out_w[...]) - noise[...]
    scale = 1.0 / (pl.num_programs(0) * residue.shape[1])
    weighted = live[...] * residue
    grad_output[...] = narrow(2.0 * weighted * scale)

    @pl.when(step == 0)
    def _():
        loss[...] = jnp.zeros_like(loss)
        total[...] = jnp.zeros_like(total)

    loss[...] += jnp.sum(weighted * residue) * scale
    product[...] = matmul(grad_output[...], out_w[...])

    def middle_back(r):
        grad = product[r, :]
        normed, inverse = normed_rows(middle[r, :])
        rights[r, columns(6)] = narrow(grad)
        rights[r, columns(7)] = narrow(grad * normed)
        grad_middle = norm_back(grad * (1.0 + modulation[r, columns(4)]), normed, inverse)
        middle[r, :] = grad_middle
        rights[r, columns(2)] = narrow(modulation[r, columns(2)] * grad_middle)
        rights[r, columns(5)] = narrow(branch[r, :] * grad_middle)

    by_rows(middle_back)
    product[...] = times_transpose(part(rights, 2)[...], part(mlp_w, 1)[...])

    def active_back(r):
        rights[r, columns(1)] = narrow(product[r, :] * silu_slope(first_pre[r, :]))

    by_rows(active_back)
    product[...] = times_transpose(part(rights, 1)[...], part(mlp_w, 0)[...])

    def first_back(r):
        grad = product[r, :]
        normed, inverse = normed_rows(start[r, :])
        rights[r, columns(3)] = narrow(grad)
        rights[r, columns(4)] = narrow(grad * normed)
        back = norm_back(grad * (1.0 + modulation[r, columns(1)]), normed, inverse)
        grad_start[r, :] = narrow(middle[r, :] + back)

    by_rows(first_back)
    product[...] = times_transpose(part(rights, 3)[...], part(wide_w, 0)[...])
    for i in range(1, 5):
        product[...] += times_transpose(part(rights, 3 + i)[...], part(wide_w, i)[...])

    def context_back(r):
        grad = product[r, :] * silu_slope(context_pre[r, :])
        rights[r, columns(0)] = narrow(grad)
        total[r, :] += grad

    by_rows(context_back)
    product[...] = times_transpose(part(rights, 0)[...], time2_w[...])

    def time_back(r):
        grad_time_pre[r, :] = narrow(product[r, :] * silu_slope(time_pre[r, :]))

    by_rows(time_back)

    @pl.when(step == pl.num_programs(0) - 1)
    def _():
        grad_cond_emb[...] = narrow(total[...])
        grad_cond[...] = narrow(times_transpose(grad_cond_emb[...], cond_w[...]))


def head_pass(noisy, noise, sinusoid, live, cond, weights):
    rows = cond.shape[0]
    flat_rows = noisy.shape[0]
    width = weights[0].shape[1]
    bf16, f32 = jnp.bfloat16, jnp.float32
    by_copy = lambda columns: pl.BlockSpec((rows, columns), lambda e: (e, 0))
    whole = lambda array: pl.BlockSpec(array.shape, lambda e: (0, 0))
    resident = pl.BlockSpec(memory_space=pltpu.VMEM)
    outs = [(flat_rows, 4 * width), (flat_rows, 8 * width), (flat_rows, width), (flat_rows, width)]
    outs += [(flat_rows, CH), (flat_rows, width), (rows, width), cond.shape]
    outs = [jax.ShapeDtypeStruct(shape, bf16) for shape in outs] + [jax.ShapeDtypeStruct((8, 128), f32)]
    out_specs = [by_copy(out.shape[1]) for out in outs[:6]] + [whole(out) for out in outs[6:]]
    flops = 6 * flat_rows * sum(weight.size for weight in weights)
    return pl.pallas_call(
        head_kernel,
        out_shape=outs,
        grid=(flat_rows // rows,),
        in_specs=[by_copy(noisy.shape[1]), by_copy(noise.shape[1]), by_copy(sinusoid.shape[1]), whole(live), whole(cond)]
        + [resident] * len(weights),
        out_specs=out_specs,
        scratch_shapes=[pltpu.VMEM((rows, width), f32)] * 7
        + [pltpu.VMEM((rows, 5 * width), f32), pltpu.VMEM((rows, width), f32)],
        compiler_params=pltpu.CompilerParams(dimension_semantics=("arbitrary",), vmem_limit_bytes=60 << 20),
        cost_estimate=pl.CostEstimate(flops=flops, bytes_accessed=60 << 20, transcendentals=flat_rows * width * 8),
    )(noisy, noise, sinusoid, live, cond, *weights)


def products_kernel(lefts, rights, mixed, out):
    unit = pl.program_id(0)

    @pl.when(unit < pl.num_programs(0) - 1)
    def _():
        size = 256

        def visit(i, carry):
            r = pl.ds(pl.multiple_of(i * size, size), size)
            out[r, :] = narrow(outer_sum(lefts[:, r], rights[...]))
            return carry

        lax.fori_loop(0, out.shape[0] // size, visit, 0)

    @pl.when(unit == pl.num_programs(0) - 1)
    def _():
        out[...] = mixed[...]


def products(lefts, rights, mixed):
    flat_rows = lefts.shape[0]
    width = mixed.shape[1]
    last_left, last_right = lefts.shape[1] // width - 1, rights.shape[1] // width - 1
    units = last_right + 2
    return pl.pallas_call(
        products_kernel,
        out_shape=jax.ShapeDtypeStruct((width, units * width), jnp.bfloat16),
        grid=(units,),
        in_specs=[
            pl.BlockSpec((flat_rows, width), lambda u: (0, jnp.minimum(u, last_left))),
            pl.BlockSpec((flat_rows, width), lambda u: (0, jnp.minimum(u, last_right))),
            pl.BlockSpec(memory_space=pltpu.VMEM),
        ],
        out_specs=pl.BlockSpec((width, width), lambda u: (0, u)),
        compiler_params=pltpu.CompilerParams(dimension_semantics=("arbitrary",), vmem_limit_bytes=40 << 20),
        cost_estimate=pl.CostEstimate(
            flops=2 * (units - 1) * flat_rows * width * width, bytes_accessed=60 << 20, transcendentals=0
        ),
    )(lefts, rights, mixed)


def head_inputs(target_rows, step_rows, noise_rows, half_freq):
    flat_rows = step_rows.size
    steps_float = step_rows.astype(jnp.float32)
    angle_noise = (steps_float / 1000.0 + 0.008) / 1.008 * (math.pi / 2)
    keep_part = jnp.cos(angle_noise) ** 2
    noisy_rows = (
        jnp.sqrt(keep_part)[:, :, None] * target_rows[None, :, :]
        + jnp.sqrt(1.0 - keep_part)[:, :, None] * noise_rows
    )
    frequency = jnp.exp(-math.log(10000.0) * jnp.arange(half_freq, dtype=jnp.float32) / half_freq)
    phases = steps_float.reshape(flat_rows, 1) * frequency[None, :]
    sinusoid = narrow(jnp.concatenate([jnp.cos(phases), jnp.sin(phases)], axis=1))
    return narrow(noisy_rows.reshape(flat_rows, CH)), sinusoid


def on_device(
    tokens,
    latents,
    orders,
    counts,
    timesteps,
    noise,
    enc_gain1,
    enc_bias1,
    enc_qkv,
    enc_proj,
    enc_gain2,
    enc_bias2,
    enc_fc1,
    enc_fc2,
    dec_gain1,
    dec_bias1,
    dec_qkv,
    dec_proj,
    dec_gain2,
    dec_bias2,
    dec_fc1,
    dec_fc2,
    mask_token,
    diff_in,
    diff_time1,
    diff_time2,
    diff_cond,
    diff_ada,
    diff_mlp1,
    diff_mlp2,
    diff_final,
    diff_out,
):
    devices = lax.axis_size("dp")
    images = tokens.shape[0]
    positions = tokens.shape[1]
    model_width = tokens.shape[2]
    tokens_here = images * L
    shard_rows = enc_proj.shape[0]
    flat_latents = latents.reshape(tokens_here, CH)
    sums_here = jnp.sum(flat_latents, axis=0)
    squares_here = jnp.sum(flat_latents * flat_latents, axis=0)
    count_here = jnp.sum(counts).astype(jnp.float32)
    statistics = jnp.concatenate([sums_here, squares_here, count_here[None]])
    vectors = [enc_gain1, enc_bias1, enc_gain2, enc_bias2, dec_gain1, dec_bias1, dec_gain2, dec_bias2, mask_token]
    statistics = jnp.concatenate(in_three(statistics))[None]
    packed = jnp.concatenate(
        [
            jnp.pad(jnp.stack(vectors, axis=1), ((0, 0), (0, 128 - len(vectors)))),
            jnp.pad(statistics, ((0, shard_rows - 1), (0, model_width - 128 - statistics.shape[1]))),
        ],
        axis=1,
    )[None]

    inner_width = diff_mlp1.shape[1]
    def feed_shard(fc1, fc2):
        return jnp.concatenate([fc1] + list(fc2.reshape(-1, shard_rows, model_width)), axis=1)

    mlp_shard = jnp.concatenate([diff_mlp1, diff_mlp2], axis=1)
    spare_rows = mlp_shard.shape[0] - shard_rows
    spare_shard = jnp.pad(mlp_shard[shard_rows:], ((0, shard_rows - spare_rows), (0, 0)))
    feed_shards = [feed_shard(enc_fc1, enc_fc2), feed_shard(dec_fc1, dec_fc2), mlp_shard[:shard_rows], spare_shard]
    ends = jnp.pad(jnp.concatenate([diff_in.T, diff_out], axis=1), ((0, 0), (0, inner_width - 2 * CH)))
    time_units = jnp.stack([diff_time2, jnp.concatenate([diff_cond, diff_time1], axis=0), ends])
    wide_units = jnp.concatenate([as_units(diff_ada, inner_width), as_units(diff_final, inner_width)], axis=0)

    qkv_kinds, proj_kinds = ((3, "columns"),), ((1, "columns"),)
    fc_count = enc_fc1.shape[1] // model_width
    late_kinds = proj_kinds + ((fc_count, "columns"), (fc_count, "rows"))

    def early_units(qkv, proj, extra):
        return jnp.concatenate([as_units(qkv, model_width), proj[None]] + extra, axis=0)

    enc_early = Gather(early_units(enc_qkv, enc_proj, [packed]), qkv_kinds + proj_kinds + proj_kinds, devices)
    dec_early = Gather(early_units(dec_qkv, dec_proj, []), qkv_kinds + proj_kinds, devices)
    head_time = Gather(time_units, ((1, "columns"),) * 3, devices)
    head_wide = Gather(wide_units, ((5, "columns"),), devices)

    gathered = lax.all_gather(jnp.concatenate(feed_shards, axis=1), "dp", axis=0, tiled=True)
    enc_early.along_upper()
    enc_early.state, dec_early.state = pin(enc_early.state, dec_early.state)
    enc_early.near()
    dec_early.along_upper()
    enc_early.state, dec_early.state = pin(enc_early.state, dec_early.state)
    enc_early.far()
    enc_early.state, dec_early.state = pin(enc_early.state, dec_early.state)
    enc_early.last()
    dec_early.near()
    enc_early.state, dec_early.state = pin(enc_early.state, dec_early.state)
    dec_early.far()
    enc_qkv_whole, enc_proj_whole, small_full = enc_early.whole()
    enc_qkv_whole, enc_proj_whole = (part.reshape(model_width, -1) for part in (enc_qkv_whole, enc_proj_whole))

    vectors = list(wide(small_full.reshape(model_width, -1)[:, :16].T))
    statistics = wide(small_full.reshape(devices, shard_rows, -1)[:, 0, 128 : 128 + 3 * (2 * CH + 1)])
    statistics = jnp.sum(jnp.sum(statistics.reshape(devices, 3, -1), axis=1), axis=0)
    sums_all, squares_all, count_all = statistics[:CH], statistics[CH : 2 * CH], statistics[2 * CH]
    cell_count = tokens_here * devices
    average = sums_all / cell_count
    spread = squares_all / cell_count - average * average
    target = ((flat_latents - average) * lax.rsqrt(spread + 1e-06)).astype(jnp.bfloat16)

    masked = (orders < counts[:, None]).astype(jnp.int32)
    flag_rows = masked.reshape(tokens_here)
    rank_rows = jnp.cumsum(flag_rows) - flag_rows
    slot_count = -(-tokens_here // devices)
    copies = timesteps.shape[1]
    drawn = jnp.concatenate(
        [noise.reshape(devices, slot_count, -1), timesteps.astype(jnp.float32).reshape(devices, slot_count, -1)], axis=2
    )
    drawn = lax.all_to_all(drawn, "dp", split_axis=0, concat_axis=0, tiled=True)
    drawn = drawn.reshape(devices * slot_count, -1)
    slots = jnp.arange(devices * slot_count, dtype=jnp.int32)
    ranks = slots % slot_count * devices + slots // slot_count
    chooser = (ranks[None, :] == rank_rows[:, None]) & (flag_rows[:, None] > 0)
    drawn = jnp.dot(
        chooser.astype(jnp.float32), drawn, precision=lax.Precision.HIGHEST, preferred_element_type=jnp.float32
    )
    noise_rows = drawn[:, : copies * CH].reshape(tokens_here, copies, CH).transpose(1, 0, 2)
    step_rows = drawn[:, copies * CH :].T

    mask_vector = vectors[8].astype(jnp.float32)

    live_keys = jnp.concatenate([jnp.ones((images, BUF), jnp.int32), 1 - masked], axis=1) > 0
    all_live = jnp.ones((images, positions), jnp.bool_)
    live_rows = live_keys.reshape(images * positions, 1)
    residual = tokens.astype(jnp.float32).reshape(images * positions, model_width)
    enc_normed, enc_projected = project_in(residual, vectors[0], vectors[1], enc_qkv_whole)
    enc_projected, dec_early.state, head_time.state = pin(enc_projected, dec_early.state, head_time.state)
    dec_early.last()
    head_time.along_upper()
    enc_log, enc_attended = attend_forward(enc_projected, live_keys, images)

    def feed_whole(first):
        unit = lambda i: gathered[:, (first + i) * model_width : (first + i + 1) * model_width]
        fc2 = [unit(fc_count + i).reshape(devices, shard_rows, -1) for i in range(fc_count)]
        fc2 = jnp.stack(fc2, axis=1)
        return gathered[:, first * model_width : (first + fc_count) * model_width], fc2.reshape(-1, model_width)

    enc_attended, dec_early.state, head_time.state, head_wide.state = pin(
        enc_attended, dec_early.state, head_time.state, head_wide.state
    )
    head_time.near()
    head_wide.along_upper()
    dec_qkv_whole, dec_proj_whole = (whole.reshape(model_width, -1) for whole in dec_early.whole())
    enc_fc1_whole, enc_fc2_whole = feed_whole(0)
    enc_feed = feed_in(residual, enc_attended, enc_proj_whole, vectors[2], vectors[3], enc_fc1_whole)
    enc_feed, dec_qkv_whole, dec_proj_whole, head_time.state = pin(
        enc_feed, dec_qkv_whole, dec_proj_whole, head_time.state
    )
    head_time.far()
    encoded = enc_feed[0] + matmul(enc_feed[3], enc_fc2_whole)
    decoder_in = jnp.where(live_rows, encoded, mask_vector[None, :])
    dec_normed, dec_projected = project_in(decoder_in, vectors[4], vectors[5], dec_qkv_whole)
    dec_projected, head_time.state, head_wide.state = pin(dec_projected, head_time.state, head_wide.state)
    head_time.last()
    head_wide.near()
    dec_log, dec_attended = attend_forward(dec_projected, all_live, images)
    dec_attended, head_time.state, head_wide.state = pin(dec_attended, head_time.state, head_wide.state)
    head_wide.far()
    time2_full, mixed, ends = (whole.reshape(-1, inner_width) for whole in head_time.whole())
    in_full, out_full = ends[:, :CH].T, ends[:, CH : 2 * CH].T
    mixed = mixed.reshape(devices, -1, inner_width)
    cond_full = mixed[:, :shard_rows].reshape(-1, inner_width)
    time1_full = mixed[:, shard_rows:].reshape(-1, inner_width)
    noisy, sinusoid = head_inputs(wide(target), step_rows, noise_rows, time1_full.shape[0] // 2)
    live_column = wide(flag_rows)[:, None]
    noise_flat = noise_rows.reshape(-1, CH)
    dec_fc1_whole, dec_fc2_whole = feed_whole(2 * fc_count)
    dec_feed = feed_in(decoder_in, dec_attended, dec_proj_whole, vectors[6], vectors[7], dec_fc1_whole)
    dec_feed, head_wide.state, in_full, out_full, cond_full, time1_full, time2_full, noisy, sinusoid = pin(
        dec_feed, head_wide.state, in_full, out_full, cond_full, time1_full, time2_full, noisy, sinusoid
    )
    head_wide.last()
    decoded = dec_feed[0] + matmul(dec_feed[3], dec_fc2_whole)
    cond_here = narrow(decoded.reshape(images, positions, model_width)[:, BUF:].reshape(tokens_here, model_width))
    wide_full = head_wide.whole()[0].reshape(-1, 5 * inner_width)
    mlp_parts = gathered[:, 4 * fc_count * model_width :].reshape(devices, shard_rows, -1)
    mlp_parts = [mlp_parts[:, :, : 2 * inner_width], mlp_parts[:, :spare_rows, 2 * inner_width :]]
    mlp_full = jnp.concatenate(mlp_parts, axis=1).reshape(inner_width, -1)
    lefts, rights, grad_time_pre, final_in, grad_output, grad_start, grad_cond_emb, grad_cond, loss_sum = head_pass(
        noisy,
        noise_flat,
        sinusoid,
        live_column,
        cond_here,
        (in_full, time1_full, time2_full, cond_full, wide_full, mlp_full, out_full),
    )
    ends = jnp.concatenate([outer_sum(noisy, grad_start), outer_sum(grad_output, final_in)], axis=0)
    loss_row = jnp.full((1, inner_width), loss_sum[0, 0], jnp.float32)
    ends = jnp.concatenate([ends, loss_row], axis=0)
    by_device = lambda part: narrow(part).reshape(devices, -1, part.shape[1])
    grad_time1, grad_cond_w = outer_sum(sinusoid, grad_time_pre), outer_sum(cond_here, grad_cond_emb)
    mixed = jnp.concatenate([by_device(grad_cond_w), by_device(grad_time1)], axis=1).reshape(-1, inner_width)
    grad_cond, diff_sum = pin(grad_cond, products(lefts, rights, mixed))
    diff_sum = lax.psum_scatter(diff_sum, "dp", scatter_dimension=0, tiled=True)
    columns_sum = lambda lo, hi: wide(diff_sum[:, lo * inner_width : hi * inner_width])
    mixed = columns_sum(8, 9)
    def scatter_late(fc1, fc2):
        fc1, fc2 = by_device(fc1), fc2.reshape(devices, -1, shard_rows, model_width)
        return Scatter([fc1, fc2], late_kinds[1:], devices)

    def scatter_early(*grads):
        return Scatter([by_device(grad) for grad in grads], qkv_kinds + proj_kinds * (len(grads) - 1), devices)

    grad_decoded = jnp.concatenate(
        [
            jnp.zeros((images, BUF, model_width), jnp.float32),
            grad_cond.astype(jnp.float32).reshape(images, L, model_width),
        ],
        axis=1,
    )
    grad_decoded = grad_decoded.reshape(images * positions, model_width)
    grad_hidden, grad_fc1, grad_fc2 = feed_backward(grad_decoded, dec_feed, dec_fc2_whole)
    grad_hidden, grad_fc1, grad_fc2, ends = pin(grad_hidden, grad_fc1, grad_fc2, ends)
    dec_late = scatter_late(grad_fc1, grad_fc2)
    ends = ends + swap(ends, 1, devices)
    grad_middle, grad_attended, grad_proj, dec_gain2_grad, dec_bias2_grad = middle_backward(
        grad_decoded, grad_hidden, dec_feed, dec_attended, vectors[6], vectors[7], dec_fc1_whole, dec_proj_whole
    )
    grad_attended, grad_proj, dec_late.state = pin(grad_attended, grad_proj, dec_late.state)
    dec_late.fold()
    grad_attended, dec_late.state = pin(grad_attended, dec_late.state)
    dec_late.near()
    grad_projected = attend_backward(grad_attended, dec_projected, dec_log, all_live, images)
    grad_qkv = narrow(outer_sum(dec_normed, grad_projected))
    grad_projected, grad_qkv, ends = pin(grad_projected, grad_qkv, ends)
    dec_early = scatter_early(grad_qkv, grad_proj)
    ends = ends + swap(ends, 2, devices)
    grad_decoder_in, dec_gain1_grad, dec_bias1_grad = inner_backward(
        grad_middle, grad_projected, decoder_in, vectors[4], vectors[5], dec_qkv_whole
    )
    grad_mask = jnp.sum(jnp.where(live_rows, 0.0, grad_decoder_in), axis=0)
    grad_encoded = jnp.where(live_rows, grad_decoder_in, 0.0)
    grad_encoded, dec_early.state = pin(grad_encoded, dec_early.state)
    dec_early.fold()
    grad_encoded, dec_early.state = pin(grad_encoded, dec_early.state)

    grad_hidden, grad_fc1, grad_fc2 = feed_backward(grad_encoded, enc_feed, enc_fc2_whole)
    grad_hidden, grad_fc1, grad_fc2, dec_late.state, ends = pin(
        grad_hidden, grad_fc1, grad_fc2, dec_late.state, ends
    )
    dec_early.near()
    ends = ends + swap(ends, 4, devices)
    enc_late = scatter_late(grad_fc1, grad_fc2)
    grad_middle, grad_attended, grad_proj, enc_gain2_grad, enc_bias2_grad = middle_backward(
        grad_encoded, grad_hidden, enc_feed, enc_attended, vectors[2], vectors[3], enc_fc1_whole, enc_proj_whole
    )
    grad_attended, grad_proj, enc_late.state = pin(grad_attended, grad_proj, enc_late.state)
    enc_late.fold()
    grad_attended, enc_late.state, dec_early.state, ends = pin(grad_attended, enc_late.state, dec_early.state, ends)
    enc_late.near()
    ends = ends + swap(ends, 8, devices)
    dec_late.far()
    grad_projected = attend_backward(grad_attended, enc_projected, enc_log, live_keys, images)
    grad_qkv = narrow(outer_sum(enc_normed, grad_projected))
    grad_residual, enc_gain1_grad, enc_bias1_grad = inner_backward(
        grad_middle, grad_projected, residual, vectors[0], vectors[1], enc_qkv_whole
    )
    grad_small = [enc_gain1_grad, enc_bias1_grad, enc_gain2_grad, enc_bias2_grad]
    grad_small += [dec_gain1_grad, dec_bias1_grad, dec_gain2_grad, dec_bias2_grad, grad_mask]
    small_count = len(grad_small)
    grad_small = jnp.stack(grad_small).T
    grad_small = jnp.pad(grad_small, ((0, 0), (0, model_width - small_count)))
    grad_residual, grad_qkv, grad_small, dec_late.state, ends = pin(
        grad_residual, grad_qkv, grad_small, dec_late.state, ends
    )
    enc_early = scatter_early(grad_qkv, grad_proj, grad_small)
    rest = 16
    while rest < devices:
        ends = ends + swap(ends, rest, devices)
        rest *= 2
    enc_early.state, enc_late.state = pin(enc_early.state, enc_late.state)
    enc_early.fold()
    enc_early.state, enc_late.state = pin(enc_early.state, enc_late.state)
    enc_early.near()
    dec_late.along_upper()
    dec_late.state, enc_early.state = pin(dec_late.state, enc_early.state)
    enc_late.far()
    dec_early.far()
    enc_late.state, dec_early.state = pin(enc_late.state, dec_early.state)
    enc_late.along_upper()
    enc_early.far()
    enc_late.state, enc_early.state = pin(enc_late.state, enc_early.state)
    enc_early.along_upper()
    dec_early.along_upper()

    def block_sums(early, late):
        early, late = early.result(), late.result()
        return [from_units(early[:3]), early[3], from_units(late[:fc_count]), late[fc_count:].reshape(-1, model_width)]

    dec_big = block_sums(dec_early, dec_late)
    enc_big = block_sums(enc_early, enc_late)
    me = lax.axis_index("dp")
    inner_rows = diff_out.shape[0]
    loss_sum = ends[2 * CH, 0]
    ends = lax.dynamic_slice_in_dim(ends[: 2 * CH], me * inner_rows, inner_rows, axis=1)
    summed = list(enc_early.result()[4][:, :small_count].T)
    enc_summed = (summed[0], summed[1], enc_big[0], enc_big[1], summed[2], summed[3], enc_big[2], enc_big[3])
    dec_summed = (summed[4], summed[5], dec_big[0], dec_big[1], summed[6], summed[7], dec_big[2], dec_big[3], summed[8])
    diff_summed = (
        ends[:CH],
        mixed[shard_rows:],
        columns_sum(0, 1),
        mixed[:shard_rows],
        columns_sum(3, 6),
        columns_sum(1, 2),
        columns_sum(2, 3),
        columns_sum(6, 8),
        ends[CH:].T,
    )
    loss_mean = loss_sum / count_all
    grad_tokens = grad_residual.reshape(images, positions, model_width)
    return (
        loss_mean,
        grad_tokens,
        enc_summed[0],
        enc_summed[1],
        enc_summed[2],
        enc_summed[3],
        enc_summed[4],
        enc_summed[5],
        enc_summed[6],
        enc_summed[7],
        dec_summed[0],
        dec_summed[1],
        dec_summed[2],
        dec_summed[3],
        dec_summed[4],
        dec_summed[5],
        dec_summed[6],
        dec_summed[7],
        dec_summed[8],
        diff_summed[0],
        diff_summed[1],
        diff_summed[2],
        diff_summed[3],
        diff_summed[4],
        diff_summed[5],
        diff_summed[6],
        diff_summed[7],
        diff_summed[8],
    )


def solution(mesh):
    placed = (
        P("dp", None, None),
        P("dp", None, None),
        P("dp", None),
        P("dp"),
        P("dp", None),
        P("dp", None, None),
        P("dp"),
        P("dp"),
        P("dp", None),
        P("dp", None),
        P("dp"),
        P("dp"),
        P("dp", None),
        P("dp", None),
        P("dp"),
        P("dp"),
        P("dp", None),
        P("dp", None),
        P("dp"),
        P("dp"),
        P("dp", None),
        P("dp", None),
        P("dp"),
        P(None, "dp"),
        P("dp", None),
        P("dp", None),
        P("dp", None),
        P("dp", None),
        P("dp", None),
        P("dp", None),
        P("dp", None),
        P("dp", None),
    )
    return jax.shard_map(
        on_device,
        mesh=mesh,
        in_specs=placed,
        out_specs=(
            P(),
            P("dp", None, None),
            P("dp"),
            P("dp"),
            P("dp", None),
            P("dp", None),
            P("dp"),
            P("dp"),
            P("dp", None),
            P("dp", None),
            P("dp"),
            P("dp"),
            P("dp", None),
            P("dp", None),
            P("dp"),
            P("dp"),
            P("dp", None),
            P("dp", None),
            P("dp"),
            P(None, "dp"),
            P("dp", None),
            P("dp", None),
            P("dp", None),
            P("dp", None),
            P("dp", None),
            P("dp", None),
            P("dp", None),
            P("dp", None),
        ),
        check_vma=False,
    )
```

```python
import functools
import math

import jax
import jax.numpy as jnp
from jax import lax
from jax.experimental import pallas as pl
from jax.experimental.pallas import tpu as pltpu
from jax.sharding import PartitionSpec as P

HEAD = 64
CH = 16
BUF = 64
L = 256


def split_masks(devices):
    bits = devices.bit_length() - 2
    upper = min(2, bits - 2)
    first = (bits - upper) // 2
    second = bits - upper - first
    group = lambda low, count: [m << low for m in range(1 << count)]
    return group(1, first), group(1 + first, second), group(1 + first + second, upper)


def swap(block, mask, devices):
    return lax.ppermute(block, "dp", [(i, i ^ mask) for i in range(devices)])


def wide(part):
    return part.astype(jnp.float32)


def narrow(part):
    return part.astype(jnp.bfloat16)


def place_kernel(layout, kinds, *refs):
    pieces = refs[: len(layout)]
    outs = refs[len(layout) : len(layout) + len(kinds)]
    sems = refs[-1]
    me = lax.axis_index("dp")
    unit = pieces[0].shape[-1]
    copies = []
    for piece, masks in zip(pieces, layout):
        for spot, mask in enumerate(masks):
            base = 0
            for out, (count, side) in zip(outs, kinds):
                for j in range(count):
                    target = out.at[me ^ mask, j]
                    if side == "columns":
                        target = out.at[me ^ mask, :, pl.ds(j * unit, unit)]
                    copies.append(
                        pltpu.make_async_copy(piece.at[spot, base + j], target, sems.at[len(copies)])
                    )
                base += count
    for copy in copies:
        copy.start()
    for copy in copies:
        copy.wait()


def whole_shape(kind, rows, unit):
    count, side = kind
    return (rows, count * unit) if side == "columns" else (count, rows, unit)


def place(pieces, layout, kinds, devices):
    _, units, rows, unit = pieces[0].shape
    dtype = pieces[0].dtype
    moved = 2 * devices * units * rows * unit * dtype.itemsize
    return pl.pallas_call(
        functools.partial(place_kernel, layout, kinds),
        out_shape=[jax.ShapeDtypeStruct((devices,) + whole_shape(kind, rows, unit), dtype) for kind in kinds],
        in_specs=[pl.BlockSpec(memory_space=pl.ANY)] * len(pieces),
        out_specs=[pl.BlockSpec(memory_space=pltpu.VMEM)] * len(kinds),
        scratch_shapes=[pltpu.SemaphoreType.DMA((devices * units,))],
        compiler_params=pltpu.CompilerParams(vmem_limit_bytes=24 << 20),
        cost_estimate=pl.CostEstimate(flops=0, bytes_accessed=moved, transcendentals=0),
    )(*pieces)


def pin(*trees):
    return lax.optimization_barrier(trees)


class Gather:
    def __init__(self, own, kinds, devices):
        self.kinds, self.devices = kinds, devices
        self.first, self.second, self.upper = split_masks(devices)
        self.state = [own]

    def beside(self):
        (own,) = self.state
        self.state = [own, swap(own, self.upper[1], self.devices)]

    def beyond(self):
        pair = jnp.stack(self.state)
        self.state = [pair, swap(pair, self.upper[2], self.devices)]

    def near(self):
        self.layout, held, self.state = [], self.state, []
        for block, base, masks in zip(held, (self.upper[:2], self.upper[2:]), (self.first, self.second)):
            self.state.append([block if m == 0 else swap(block, m, self.devices) for m in masks])
            self.layout.append([m ^ v for m in masks for v in base])

    def far(self):
        self.state = [jnp.concatenate(blocks, axis=0) for blocks in self.state]
        for block, base, masks in zip(self.state[:2], self.layout[:2], (self.second, self.first)):
            for m in masks[1:]:
                self.state.append(swap(block, m, self.devices))
                self.layout.append([m ^ v for v in base])
        self.across(0, 2)

    def across(self, start, stop):
        self.state += [swap(block, 1, self.devices) for block in self.state[start:stop]]
        self.layout += [[1 ^ v for v in base] for base in self.layout[start:stop]]

    def last(self):
        self.across(2, len(self.state) - 2)

    def whole(self):
        return place(self.state, self.layout, self.kinds, self.devices)


def as_units(shard, unit):
    rows, width = shard.shape
    return shard.reshape(rows, width // unit, unit).transpose(1, 0, 2)


def fold_kernel(sizes, kinds, table, *refs):
    count = len(kinds)
    mine, theirs, outs = refs[:count], refs[count : 2 * count], refs[2 * count :]
    step = pl.program_id(0)
    start = 0
    for out, size in zip(outs, sizes):
        unit = out.shape[-1]

        @pl.when((step >= start) & (step < start + size))
        def _(out=out, unit=unit):
            base = 0
            for own, other, (units, side) in zip(mine, theirs, kinds):
                for j in range(units):
                    spot = (0, j) if side == "rows" else (0, slice(None), slice(j * unit, (j + 1) * unit))
                    out[0, base + j] = narrow(wide(own[spot]) + wide(other[spot]))
                base += units

        start += size


def fold(mine, theirs, kinds, slots, devices):
    unit = theirs[0].shape[-1] // (kinds[0][0] if kinds[0][1] == "columns" else 1)
    rows = theirs[0].shape[-2]
    units = sum(count for count, _ in kinds)
    sizes = [len(group) for group in slots]
    me = lax.axis_index("dp")
    order = jnp.asarray([chip for group in slots for chip in group], jnp.int32)
    table = (me // 2) ^ order
    table = jnp.concatenate([table, (me % 2).reshape(1).astype(jnp.int32)])
    total = len(order)
    zeros = lambda array: (0,) * (array.ndim - 1)
    own_spec = lambda a: pl.BlockSpec((1,) + a.shape[1:], lambda s, t, z=zeros(a): (t[s] * 2 + t[total],) + z)
    other_spec = lambda a: pl.BlockSpec((1,) + a.shape[1:], lambda s, t, z=zeros(a): (t[s],) + z)
    out_specs, start = [], 0
    for size in sizes:
        out_specs.append(
            pl.BlockSpec(
                (1, units, rows, unit), lambda s, t, lo=start, top=size - 1: (jnp.clip(s - lo, 0, top), 0, 0, 0)
            )
        )
        start += size
    moved = 3 * total * units * rows * unit * 2
    return pl.pallas_call(
        functools.partial(fold_kernel, sizes, kinds),
        out_shape=[jax.ShapeDtypeStruct((size, units, rows, unit), jnp.bfloat16) for size in sizes],
        grid_spec=pltpu.PrefetchScalarGridSpec(
            num_scalar_prefetch=1,
            grid=(total,),
            in_specs=[own_spec(a) for a in mine] + [other_spec(a) for a in theirs],
            out_specs=out_specs,
        ),
        compiler_params=pltpu.CompilerParams(
            dimension_semantics=("arbitrary",), vmem_limit_bytes=32 << 20
        ),
        cost_estimate=pl.CostEstimate(flops=moved, bytes_accessed=moved, transcendentals=0),
    )(table, *mine, *theirs)


class Scatter:
    def __init__(self, wholes, kinds, devices):
        self.kinds, self.devices, self.wholes = kinds, devices, wholes
        first, second, upper = ([m // 2 for m in masks] for masks in split_masks(devices))
        half = len(upper) // 2
        self.upper = upper
        self.routes = ((upper[:half], second, first), (upper[half:], first, second))
        core = lax.axis_index("dp") % 2
        self.state = []
        for whole in wholes:
            pairs = whole.reshape((devices // 2, 2) + whole.shape[1:])
            self.state.append(swap(lax.dynamic_index_in_dim(pairs, 1 - core, 1, keepdims=False), 1, devices))

    def fold(self):
        slots = [[u ^ n ^ f for f in far for u in ups] for ups, near, far in self.routes for n in near]
        self.state = fold(self.wholes, self.state, self.kinds, slots, self.devices)
        self.wholes = None

    def near(self):
        masks = [n for _, near, _ in self.routes for n in near]
        self.state = [g if n == 0 else swap(g, 2 * n, self.devices) for g, n in zip(self.state, masks)]

    def far(self):
        held, self.state = self.state, []
        for ups, near, far in self.routes:
            groups, held = held[: len(near)], held[len(near) :]
            blocks = [wide(g).reshape((len(far), len(ups)) + g.shape[1:]) for g in groups]
            for spot, f in enumerate(far):
                total = blocks[0][spot]
                for block in blocks[1:]:
                    total = total + block[spot]
                total = narrow(total)
                self.state.append(total if f == 0 else swap(total, 2 * f, self.devices))

    def along_upper(self):
        held, parts = self.state, []
        for ups, near, far in self.routes:
            groups, held = held[: len(far)], held[len(far) :]
            for spot in range(len(ups)):
                total = wide(groups[0][spot])
                for g in groups[1:]:
                    total = total + wide(g[spot])
                parts.append(narrow(total))
        self.state = [p if u == 0 else swap(p, 2 * u, self.devices) for p, u in zip(parts, self.upper)]

    def result(self):
        total = wide(self.state[0])
        for part in self.state[1:]:
            total = total + wide(part)
        return total


def from_units(units):
    count, rows, unit = units.shape
    return units.transpose(1, 0, 2).reshape(rows, count * unit)


def sum_all(block, devices):
    mask = 1
    while mask < devices:
        block = block + swap(block, mask, devices)
        mask *= 2
    return block


def in_three(values):
    first = lax.reduce_precision(values, 8, 7)
    second = lax.reduce_precision(values - first, 8, 7)
    third = values - first - second
    return [narrow(part) for part in (first, second, third)]


def layer_norm(residual, gain, offset):
    centred = residual - jnp.mean(residual, axis=-1, keepdims=True)
    spread = jnp.mean(centred * centred, axis=-1, keepdims=True)
    return centred * lax.rsqrt(spread + 1e-06) * gain + offset


def plain_norm(residual):
    centred = residual - jnp.mean(residual, axis=-1, keepdims=True)
    spread = jnp.mean(centred * centred, axis=-1, keepdims=True)
    return centred * lax.rsqrt(spread + 1e-06)


def modulate(residual, shift_part, scale_part):
    return plain_norm(residual) * (1.0 + scale_part) + shift_part


def exact_gelu(hidden):
    below = 0.5 + 0.5 * lax.erf(hidden * math.sqrt(0.5))
    density = jnp.exp(-0.5 * hidden * hidden) * (1.0 / math.sqrt(2.0 * math.pi))
    return hidden * below, below + hidden * density


def matmul(left, right):
    return jnp.dot(left, right, preferred_element_type=jnp.float32)


def outer_sum(left, right):
    return lax.dot_general(
        left, right, (((0,), (0,)), ((), ())), preferred_element_type=jnp.float32
    )


def times_transpose(left, right):
    return lax.dot_general(
        left, right, (((1,), (1,)), ((), ())), preferred_element_type=jnp.float32
    )


def attention_scores(query_rows, key_rows, keys_live):
    scores = jnp.einsum(
        "bqhe,bkhe->bhqk", query_rows, key_rows, preferred_element_type=jnp.float32
    ) * HEAD ** (-0.5)
    return jnp.where(keys_live[:, None, None, :], scores, -1e30)


def split_heads(projected, images):
    positions = projected.shape[0] // images
    head_count = projected.shape[1] // (3 * HEAD)
    shaped = projected.reshape(images, positions, 3, head_count, HEAD)
    return (shaped[:, :, 0], shaped[:, :, 1], shaped[:, :, 2])


def project_in(residual, gain, offset, qkv_w):
    normed = narrow(layer_norm(residual, wide(gain), wide(offset)))
    return normed, narrow(matmul(normed, qkv_w))


def attend_forward(projected, keys_live, images):
    query_rows, key_rows, value_rows = split_heads(projected, images)
    scores = attention_scores(query_rows, key_rows, keys_live)
    row_peak = jnp.max(scores, axis=-1, keepdims=True)
    log_total = row_peak + jnp.log(jnp.sum(jnp.exp(scores - row_peak), axis=-1, keepdims=True))
    soft_rounded = narrow(jnp.exp(scores - log_total))
    attended = jnp.einsum("bhqk,bkhe->bqhe", soft_rounded, value_rows, preferred_element_type=jnp.float32)
    return log_total, narrow(attended).reshape(projected.shape[0], -1)


def feed_in(residual, attended, proj_w, gain, offset, fc1_w):
    middle = residual + matmul(attended, proj_w)
    normed = narrow(layer_norm(middle, wide(gain), wide(offset)))
    active, slope = exact_gelu(matmul(normed, fc1_w))
    return middle, normed, slope, narrow(active)


def feed_backward(grad_output, saved, fc2_w):
    _, normed, slope, active = saved
    grad_branch = narrow(grad_output)
    grad_active = times_transpose(grad_branch, fc2_w)
    grad_hidden = narrow(grad_active * slope)
    return grad_hidden, narrow(outer_sum(normed, grad_hidden)), narrow(outer_sum(active, grad_branch))


def middle_backward(grad_output, grad_hidden, saved, attended, gain, offset, fc1_w, proj_w):
    grad_normed = times_transpose(grad_hidden, fc1_w)
    back = jax.vjp(layer_norm, saved[0], wide(gain), wide(offset))[1]
    grad_norm, grad_gain, grad_offset = back(grad_normed)
    grad_middle = grad_output + grad_norm
    grad_attention = narrow(grad_middle)
    grad_proj = narrow(outer_sum(attended, grad_attention))
    grad_attended = narrow(times_transpose(grad_attention, proj_w))
    return grad_middle, grad_attended, grad_proj, grad_gain, grad_offset


def attend_backward(grad_attended, projected, log_total, keys_live, images):
    rows, model_width = grad_attended.shape
    grad_attended = grad_attended.reshape(images, rows // images, model_width // HEAD, HEAD)
    query_rows, key_rows, value_rows = split_heads(projected, images)
    scores = attention_scores(query_rows, key_rows, keys_live)
    soft_full = jnp.exp(scores - log_total)
    soft_rounded = narrow(soft_full)
    grad_value = jnp.einsum("bhqk,bqhe->bkhe", soft_rounded, grad_attended, preferred_element_type=jnp.float32)
    grad_soft = jnp.einsum("bqhe,bkhe->bhqk", grad_attended, value_rows, preferred_element_type=jnp.float32)
    grad_scores = soft_full * (grad_soft - jnp.sum(grad_soft * soft_full, axis=-1, keepdims=True))
    grad_scores = narrow(grad_scores)
    grad_query = jnp.einsum(
        "bhqk,bkhe->bqhe", grad_scores, key_rows, preferred_element_type=jnp.float32
    ) * HEAD ** (-0.5)
    grad_key = jnp.einsum(
        "bhqk,bqhe->bkhe", grad_scores, query_rows, preferred_element_type=jnp.float32
    ) * HEAD ** (-0.5)
    grad_projected = narrow(jnp.stack([grad_query, grad_key, grad_value], axis=2))
    return grad_projected.reshape(rows, 3 * model_width)


def inner_backward(grad_middle, grad_projected, residual, gain, offset, qkv_w):
    grad_normed = times_transpose(grad_projected, qkv_w)
    back = jax.vjp(layer_norm, residual, wide(gain), wide(offset))[1]
    grad_norm, grad_gain, grad_offset = back(grad_normed)
    return grad_middle + grad_norm, grad_gain, grad_offset


def silu_slope(value):
    gate = jax.nn.sigmoid(value)
    return gate * (1.0 + value * (1.0 - gate))


def normed_rows(value):
    centred = value - jnp.mean(value, axis=-1, keepdims=True)
    inverse = lax.rsqrt(jnp.mean(centred * centred, axis=-1, keepdims=True) + 1e-06)
    return centred * inverse, inverse


def norm_back(grad, normed, inverse):
    spread = jnp.mean(grad * normed, axis=-1, keepdims=True)
    return inverse * (grad - jnp.mean(grad, axis=-1, keepdims=True) - normed * spread)


def head_kernel(
    noisy, noise, sinusoid, live, cond, in_w, time1_w, time2_w, cond_w, wide_w, mlp_w, out_w,
    lefts, rights, grad_time_pre, final_in, grad_output, grad_start, grad_cond_emb, grad_cond, loss,
    time_pre, context_pre, start, first_pre, branch, middle, product, modulation, total,
):
    step = pl.program_id(0)
    rows, width = time_pre.shape
    part = lambda array, i, count=1: array.at[:, i * width : (i + count) * width]

    def by_rows(body):
        body(pl.ds(0, rows))

    def columns(i):
        return slice(i * width, (i + 1) * width)

    time_pre[...] = matmul(sinusoid[...], time1_w[...])

    def time_rows(r):
        lefts[r, columns(0)] = narrow(jax.nn.silu(time_pre[r, :]))

    by_rows(time_rows)
    context_pre[...] = matmul(part(lefts, 0)[...], time2_w[...]) + matmul(cond[...], cond_w[...])

    def context_rows(r):
        lefts[r, columns(3)] = narrow(jax.nn.silu(context_pre[r, :]))

    by_rows(context_rows)
    for i in range(5):
        part(modulation, i)[...] = matmul(part(lefts, 3)[...], part(wide_w, i)[...])
    start[...] = matmul(noisy[...], in_w[...])

    def first_rows(r):
        normed, _ = normed_rows(start[r, :])
        lefts[r, columns(1)] = narrow(normed * (1.0 + modulation[r, columns(1)]) + modulation[r, columns(0)])

    by_rows(first_rows)
    first_pre[...] = matmul(part(lefts, 1)[...], part(mlp_w, 0)[...])

    def active_rows(r):
        lefts[r, columns(2)] = narrow(jax.nn.silu(first_pre[r, :]))

    by_rows(active_rows)
    branch[...] = matmul(part(lefts, 2)[...], part(mlp_w, 1)[...])

    def middle_rows(r):
        value = start[r, :] + modulation[r, columns(2)] * branch[r, :]
        middle[r, :] = value
        normed, _ = normed_rows(value)
        final_in[r, :] = narrow(normed * (1.0 + modulation[r, columns(4)]) + modulation[r, columns(3)])

    by_rows(middle_rows)
    residue = times_transpose(final_in[...], out_w[...]) - noise[...]
    scale = 1.0 / (pl.num_programs(0) * residue.shape[1])
    weighted = live[...] * residue
    grad_output[...] = narrow(2.0 * weighted * scale)

    @pl.when(step == 0)
    def _():
        loss[...] = jnp.zeros_like(loss)
        total[...] = jnp.zeros_like(total)

    loss[...] += jnp.sum(weighted * residue) * scale
    product[...] = matmul(grad_output[...], out_w[...])

    def middle_back(r):
        grad = product[r, :]
        normed, inverse = normed_rows(middle[r, :])
        rights[r, columns(6)] = narrow(grad)
        rights[r, columns(7)] = narrow(grad * normed)
        grad_middle = norm_back(grad * (1.0 + modulation[r, columns(4)]), normed, inverse)
        middle[r, :] = grad_middle
        rights[r, columns(2)] = narrow(modulation[r, columns(2)] * grad_middle)
        rights[r, columns(5)] = narrow(branch[r, :] * grad_middle)

    by_rows(middle_back)
    product[...] = times_transpose(part(rights, 2)[...], part(mlp_w, 1)[...])

    def active_back(r):
        rights[r, columns(1)] = narrow(product[r, :] * silu_slope(first_pre[r, :]))

    by_rows(active_back)
    product[...] = times_transpose(part(rights, 1)[...], part(mlp_w, 0)[...])

    def first_back(r):
        grad = product[r, :]
        normed, inverse = normed_rows(start[r, :])
        rights[r, columns(3)] = narrow(grad)
        rights[r, columns(4)] = narrow(grad * normed)
        back = norm_back(grad * (1.0 + modulation[r, columns(1)]), normed, inverse)
        grad_start[r, :] = narrow(middle[r, :] + back)

    by_rows(first_back)
    product[...] = times_transpose(part(rights, 3)[...], part(wide_w, 0)[...])
    for i in range(1, 5):
        product[...] += times_transpose(part(rights, 3 + i)[...], part(wide_w, i)[...])

    def context_back(r):
        grad = product[r, :] * silu_slope(context_pre[r, :])
        rights[r, columns(0)] = narrow(grad)
        total[r, :] += grad

    by_rows(context_back)
    product[...] = times_transpose(part(rights, 0)[...], time2_w[...])

    def time_back(r):
        grad_time_pre[r, :] = narrow(product[r, :] * silu_slope(time_pre[r, :]))

    by_rows(time_back)

    @pl.when(step == pl.num_programs(0) - 1)
    def _():
        grad_cond_emb[...] = narrow(total[...])
        grad_cond[...] = narrow(times_transpose(grad_cond_emb[...], cond_w[...]))


def head_pass(noisy, noise, sinusoid, live, cond, weights):
    rows = cond.shape[0]
    flat_rows = noisy.shape[0]
    width = weights[0].shape[1]
    bf16, f32 = jnp.bfloat16, jnp.float32
    by_copy = lambda columns: pl.BlockSpec((rows, columns), lambda e: (e, 0))
    whole = lambda array: pl.BlockSpec(array.shape, lambda e: (0, 0))
    resident = pl.BlockSpec(memory_space=pltpu.VMEM)
    outs = [(flat_rows, 4 * width), (flat_rows, 8 * width), (flat_rows, width), (flat_rows, width)]
    outs += [(flat_rows, CH), (flat_rows, width), (rows, width), cond.shape]
    outs = [jax.ShapeDtypeStruct(shape, bf16) for shape in outs] + [jax.ShapeDtypeStruct((8, 128), f32)]
    out_specs = [by_copy(out.shape[1]) for out in outs[:6]] + [whole(out) for out in outs[6:]]
    flops = 6 * flat_rows * sum(weight.size for weight in weights)
    return pl.pallas_call(
        head_kernel,
        out_shape=outs,
        grid=(flat_rows // rows,),
        in_specs=[by_copy(noisy.shape[1]), by_copy(noise.shape[1]), by_copy(sinusoid.shape[1]), whole(live), whole(cond)]
        + [resident] * len(weights),
        out_specs=out_specs,
        scratch_shapes=[pltpu.VMEM((rows, width), f32)] * 7
        + [pltpu.VMEM((rows, 5 * width), f32), pltpu.VMEM((rows, width), f32)],
        compiler_params=pltpu.CompilerParams(dimension_semantics=("arbitrary",), vmem_limit_bytes=60 << 20),
        cost_estimate=pl.CostEstimate(flops=flops, bytes_accessed=60 << 20, transcendentals=flat_rows * width * 8),
    )(noisy, noise, sinusoid, live, cond, *weights)


def products_kernel(lefts, rights, mixed, out):
    unit = pl.program_id(0)

    @pl.when(unit < pl.num_programs(0) - 1)
    def _():
        size = 256

        def visit(i, carry):
            r = pl.ds(pl.multiple_of(i * size, size), size)
            out[r, :] = narrow(outer_sum(lefts[:, r], rights[...]))
            return carry

        lax.fori_loop(0, out.shape[0] // size, visit, 0, unroll=True)

    @pl.when(unit == pl.num_programs(0) - 1)
    def _():
        out[...] = mixed[...]


def products(lefts, rights, mixed):
    flat_rows = lefts.shape[0]
    width = mixed.shape[1]
    last_left, last_right = lefts.shape[1] // width - 1, rights.shape[1] // width - 1
    units = last_right + 2
    return pl.pallas_call(
        products_kernel,
        out_shape=jax.ShapeDtypeStruct((width, units * width), jnp.bfloat16),
        grid=(units,),
        in_specs=[
            pl.BlockSpec((flat_rows, width), lambda u: (0, jnp.minimum(u, last_left))),
            pl.BlockSpec((flat_rows, width), lambda u: (0, jnp.minimum(u, last_right))),
            pl.BlockSpec(memory_space=pltpu.VMEM),
        ],
        out_specs=pl.BlockSpec((width, width), lambda u: (0, u)),
        compiler_params=pltpu.CompilerParams(dimension_semantics=("arbitrary",), vmem_limit_bytes=40 << 20),
        cost_estimate=pl.CostEstimate(
            flops=2 * (units - 1) * flat_rows * width * width, bytes_accessed=60 << 20, transcendentals=0
        ),
    )(lefts, rights, mixed)


def head_inputs(target_rows, step_rows, noise_rows, half_freq):
    flat_rows = step_rows.size
    steps_float = step_rows.astype(jnp.float32)
    angle_noise = (steps_float / 1000.0 + 0.008) / 1.008 * (math.pi / 2)
    keep_part = jnp.cos(angle_noise) ** 2
    noisy_rows = (
        jnp.sqrt(keep_part)[:, :, None] * target_rows[None, :, :]
        + jnp.sqrt(1.0 - keep_part)[:, :, None] * noise_rows
    )
    frequency = jnp.exp(-math.log(10000.0) * jnp.arange(half_freq, dtype=jnp.float32) / half_freq)
    phases = steps_float.reshape(flat_rows, 1) * frequency[None, :]
    sinusoid = narrow(jnp.concatenate([jnp.cos(phases), jnp.sin(phases)], axis=1))
    return narrow(noisy_rows.reshape(flat_rows, CH)), sinusoid


def on_device(
    tokens,
    latents,
    orders,
    counts,
    timesteps,
    noise,
    enc_gain1,
    enc_bias1,
    enc_qkv,
    enc_proj,
    enc_gain2,
    enc_bias2,
    enc_fc1,
    enc_fc2,
    dec_gain1,
    dec_bias1,
    dec_qkv,
    dec_proj,
    dec_gain2,
    dec_bias2,
    dec_fc1,
    dec_fc2,
    mask_token,
    diff_in,
    diff_time1,
    diff_time2,
    diff_cond,
    diff_ada,
    diff_mlp1,
    diff_mlp2,
    diff_final,
    diff_out,
):
    devices = lax.axis_size("dp")
    images = tokens.shape[0]
    positions = tokens.shape[1]
    model_width = tokens.shape[2]
    tokens_here = images * L
    shard_rows = enc_proj.shape[0]
    flat_latents = latents.reshape(tokens_here, CH)
    sums_here = jnp.sum(flat_latents, axis=0)
    squares_here = jnp.sum(flat_latents * flat_latents, axis=0)
    count_here = jnp.sum(counts).astype(jnp.float32)
    statistics = jnp.concatenate([sums_here, squares_here, count_here[None]])
    vectors = [enc_gain1, enc_bias1, enc_gain2, enc_bias2, dec_gain1, dec_bias1, dec_gain2, dec_bias2, mask_token]
    statistics = jnp.concatenate(in_three(statistics))[None]
    packed = jnp.concatenate(
        [
            jnp.pad(jnp.stack(vectors, axis=1), ((0, 0), (0, 128 - len(vectors)))),
            jnp.pad(statistics, ((0, shard_rows - 1), (0, model_width - 128 - statistics.shape[1]))),
        ],
        axis=1,
    )[None]

    inner_width = diff_mlp1.shape[1]
    def feed_shard(fc1, fc2):
        return jnp.concatenate([fc1] + list(fc2.reshape(-1, shard_rows, model_width)), axis=1)

    mlp_shard = jnp.concatenate([diff_mlp1, diff_mlp2], axis=1)
    spare_rows = mlp_shard.shape[0] - shard_rows
    spare_shard = jnp.pad(mlp_shard[shard_rows:], ((0, shard_rows - spare_rows), (0, 0)))
    feed_shards = [feed_shard(enc_fc1, enc_fc2), feed_shard(dec_fc1, dec_fc2), mlp_shard[:shard_rows], spare_shard]
    ends = jnp.pad(jnp.concatenate([diff_in.T, diff_out], axis=1), ((0, 0), (0, inner_width - 2 * CH)))
    time_units = jnp.stack([diff_time2, jnp.concatenate([diff_cond, diff_time1], axis=0), ends])
    wide_units = jnp.concatenate([as_units(diff_ada, inner_width), as_units(diff_final, inner_width)], axis=0)

    qkv_kinds, proj_kinds = ((3, "columns"),), ((1, "columns"),)
    fc_count = enc_fc1.shape[1] // model_width
    late_kinds = proj_kinds + ((fc_count, "columns"), (fc_count, "rows"))

    def early_units(qkv, proj, extra):
        return jnp.concatenate([as_units(qkv, model_width), proj[None]] + extra, axis=0)

    enc_early = Gather(early_units(enc_qkv, enc_proj, [packed]), qkv_kinds + proj_kinds + proj_kinds, devices)
    dec_early = Gather(early_units(dec_qkv, dec_proj, []), qkv_kinds + proj_kinds, devices)
    head_time = Gather(time_units, ((1, "columns"),) * 3, devices)
    head_wide = Gather(wide_units, ((5, "columns"),), devices)

    gathered = lax.all_gather(jnp.concatenate(feed_shards, axis=1), "dp", axis=0, tiled=True)
    enc_early.beside()
    (enc_early.state,) = pin(enc_early.state)
    enc_early.beyond()
    enc_early.state, dec_early.state = pin(enc_early.state, dec_early.state)
    enc_early.near()
    dec_early.beside()
    enc_early.state, dec_early.state = pin(enc_early.state, dec_early.state)
    enc_early.far()
    dec_early.beyond()
    enc_early.state, dec_early.state, head_time.state = pin(enc_early.state, dec_early.state, head_time.state)
    enc_early.last()
    dec_early.near()
    head_time.beside()
    enc_early.state, dec_early.state, head_time.state = pin(enc_early.state, dec_early.state, head_time.state)
    dec_early.far()
    head_time.beyond()
    enc_qkv_whole, enc_proj_whole, small_full = enc_early.whole()
    enc_qkv_whole, enc_proj_whole = (part.reshape(model_width, -1) for part in (enc_qkv_whole, enc_proj_whole))

    vectors = list(wide(small_full.reshape(model_width, -1)[:, :16].T))
    statistics = wide(small_full.reshape(devices, shard_rows, -1)[:, 0, 128 : 128 + 3 * (2 * CH + 1)])
    statistics = jnp.sum(jnp.sum(statistics.reshape(devices, 3, -1), axis=1), axis=0)
    sums_all, squares_all, count_all = statistics[:CH], statistics[CH : 2 * CH], statistics[2 * CH]
    cell_count = tokens_here * devices
    average = sums_all / cell_count
    spread = squares_all / cell_count - average * average
    target = ((flat_latents - average) * lax.rsqrt(spread + 1e-06)).astype(jnp.bfloat16)

    masked = (orders < counts[:, None]).astype(jnp.int32)
    flag_rows = masked.reshape(tokens_here)
    rank_rows = jnp.cumsum(flag_rows) - flag_rows
    slot_count = -(-tokens_here // devices)
    copies = timesteps.shape[1]
    drawn = jnp.concatenate(
        [noise.reshape(devices, slot_count, -1), timesteps.astype(jnp.float32).reshape(devices, slot_count, -1)], axis=2
    )
    drawn = lax.all_to_all(drawn, "dp", split_axis=0, concat_axis=0, tiled=True)
    drawn = drawn.reshape(devices * slot_count, -1)
    slots = jnp.arange(devices * slot_count, dtype=jnp.int32)
    ranks = slots % slot_count * devices + slots // slot_count
    chooser = (ranks[None, :] == rank_rows[:, None]) & (flag_rows[:, None] > 0)
    drawn = jnp.dot(
        chooser.astype(jnp.float32), drawn, precision=lax.Precision.HIGHEST, preferred_element_type=jnp.float32
    )
    noise_rows = drawn[:, : copies * CH].reshape(tokens_here, copies, CH).transpose(1, 0, 2)
    step_rows = drawn[:, copies * CH :].T

    mask_vector = vectors[8].astype(jnp.float32)

    live_keys = jnp.concatenate([jnp.ones((images, BUF), jnp.int32), 1 - masked], axis=1) > 0
    all_live = jnp.ones((images, positions), jnp.bool_)
    live_rows = live_keys.reshape(images * positions, 1)
    residual = tokens.astype(jnp.float32).reshape(images * positions, model_width)
    enc_normed, enc_projected = project_in(residual, vectors[0], vectors[1], enc_qkv_whole)
    enc_projected, dec_early.state, head_time.state, head_wide.state = pin(
        enc_projected, dec_early.state, head_time.state, head_wide.state
    )
    dec_early.last()
    head_time.near()
    head_wide.beside()
    enc_log, enc_attended = attend_forward(enc_projected, live_keys, images)

    def feed_whole(first):
        unit = lambda i: gathered[:, (first + i) * model_width : (first + i + 1) * model_width]
        fc2 = [unit(fc_count + i).reshape(devices, shard_rows, -1) for i in range(fc_count)]
        fc2 = jnp.stack(fc2, axis=1)
        return gathered[:, first * model_width : (first + fc_count) * model_width], fc2.reshape(-1, model_width)

    enc_attended, dec_early.state, head_time.state, head_wide.state = pin(
        enc_attended, dec_early.state, head_time.state, head_wide.state
    )
    head_time.far()
    head_wide.beyond()
    dec_qkv_whole, dec_proj_whole = (whole.reshape(model_width, -1) for whole in dec_early.whole())
    enc_attended, dec_qkv_whole, dec_proj_whole = pin(enc_attended, dec_qkv_whole, dec_proj_whole)
    enc_fc1_whole, enc_fc2_whole = feed_whole(0)
    enc_feed = feed_in(residual, enc_attended, enc_proj_whole, vectors[2], vectors[3], enc_fc1_whole)
    enc_feed, dec_qkv_whole, dec_proj_whole, head_time.state, head_wide.state = pin(
        enc_feed, dec_qkv_whole, dec_proj_whole, head_time.state, head_wide.state
    )
    head_time.last()
    head_wide.near()
    encoded = enc_feed[0] + matmul(enc_feed[3], enc_fc2_whole)
    decoder_in = jnp.where(live_rows, encoded, mask_vector[None, :])
    dec_normed, dec_projected = project_in(decoder_in, vectors[4], vectors[5], dec_qkv_whole)
    dec_projected, head_time.state, head_wide.state = pin(dec_projected, head_time.state, head_wide.state)
    head_wide.far()
    dec_log, dec_attended = attend_forward(dec_projected, all_live, images)
    dec_attended, head_wide.state = pin(dec_attended, head_wide.state)
    head_wide.last()
    time2_full, mixed, ends = (whole.reshape(-1, inner_width) for whole in head_time.whole())
    in_full, out_full = ends[:, :CH].T, ends[:, CH : 2 * CH].T
    mixed = mixed.reshape(devices, -1, inner_width)
    cond_full = mixed[:, :shard_rows].reshape(-1, inner_width)
    time1_full = mixed[:, shard_rows:].reshape(-1, inner_width)
    noisy, sinusoid = head_inputs(wide(target), step_rows, noise_rows, time1_full.shape[0] // 2)
    live_column = wide(flag_rows)[:, None]
    noise_flat = noise_rows.reshape(-1, CH)
    dec_fc1_whole, dec_fc2_whole = feed_whole(2 * fc_count)
    dec_feed = feed_in(decoder_in, dec_attended, dec_proj_whole, vectors[6], vectors[7], dec_fc1_whole)
    dec_feed, in_full, out_full, cond_full, time1_full, time2_full, noisy, sinusoid = pin(
        dec_feed, in_full, out_full, cond_full, time1_full, time2_full, noisy, sinusoid
    )
    decoded = dec_feed[0] + matmul(dec_feed[3], dec_fc2_whole)
    cond_here = narrow(decoded.reshape(images, positions, model_width)[:, BUF:].reshape(tokens_here, model_width))
    wide_full = head_wide.whole()[0].reshape(-1, 5 * inner_width)
    mlp_parts = gathered[:, 4 * fc_count * model_width :].reshape(devices, shard_rows, -1)
    mlp_parts = [mlp_parts[:, :, : 2 * inner_width], mlp_parts[:, :spare_rows, 2 * inner_width :]]
    mlp_full = jnp.concatenate(mlp_parts, axis=1).reshape(inner_width, -1)
    lefts, rights, grad_time_pre, final_in, grad_output, grad_start, grad_cond_emb, grad_cond, loss_sum = head_pass(
        noisy,
        noise_flat,
        sinusoid,
        live_column,
        cond_here,
        (in_full, time1_full, time2_full, cond_full, wide_full, mlp_full, out_full),
    )
    ends = jnp.concatenate([outer_sum(noisy, grad_start), outer_sum(grad_output, final_in)], axis=0)
    loss_row = jnp.full((1, inner_width), loss_sum[0, 0], jnp.float32)
    ends = jnp.concatenate([ends, loss_row], axis=0)
    by_device = lambda part: narrow(part).reshape(devices, -1, part.shape[1])
    grad_time1, grad_cond_w = outer_sum(sinusoid, grad_time_pre), outer_sum(cond_here, grad_cond_emb)
    mixed = jnp.concatenate([by_device(grad_cond_w), by_device(grad_time1)], axis=1).reshape(-1, inner_width)
    grad_cond, diff_sum = pin(grad_cond, products(lefts, rights, mixed))
    diff_sum = lax.psum_scatter(diff_sum, "dp", scatter_dimension=0, tiled=True)
    columns_sum = lambda lo, hi: wide(diff_sum[:, lo * inner_width : hi * inner_width])
    mixed = columns_sum(8, 9)
    def scatter_late(fc1, fc2):
        fc1, fc2 = by_device(fc1), fc2.reshape(devices, -1, shard_rows, model_width)
        return Scatter([fc1, fc2], late_kinds[1:], devices)

    def scatter_early(*grads):
        return Scatter([by_device(grad) for grad in grads], qkv_kinds + proj_kinds * (len(grads) - 1), devices)

    grad_decoded = jnp.concatenate(
        [
            jnp.zeros((images, BUF, model_width), jnp.float32),
            grad_cond.astype(jnp.float32).reshape(images, L, model_width),
        ],
        axis=1,
    )
    grad_decoded = grad_decoded.reshape(images * positions, model_width)
    grad_hidden, grad_fc1, grad_fc2 = feed_backward(grad_decoded, dec_feed, dec_fc2_whole)
    grad_hidden, grad_fc1, grad_fc2, ends = pin(grad_hidden, grad_fc1, grad_fc2, ends)
    dec_late = scatter_late(grad_fc1, grad_fc2)
    ends = ends + swap(ends, 1, devices)
    grad_middle, grad_attended, grad_proj, dec_gain2_grad, dec_bias2_grad = middle_backward(
        grad_decoded, grad_hidden, dec_feed, dec_attended, vectors[6], vectors[7], dec_fc1_whole, dec_proj_whole
    )
    grad_attended, grad_proj, dec_late.state = pin(grad_attended, grad_proj, dec_late.state)
    dec_late.fold()
    grad_attended, dec_late.state = pin(grad_attended, dec_late.state)
    dec_late.near()
    grad_projected = attend_backward(grad_attended, dec_projected, dec_log, all_live, images)
    grad_qkv = narrow(outer_sum(dec_normed, grad_projected))
    grad_projected, grad_qkv, ends = pin(grad_projected, grad_qkv, ends)
    dec_early = scatter_early(grad_qkv, grad_proj)
    ends = ends + swap(ends, 2, devices)
    grad_decoder_in, dec_gain1_grad, dec_bias1_grad = inner_backward(
        grad_middle, grad_projected, decoder_in, vectors[4], vectors[5], dec_qkv_whole
    )
    grad_mask = jnp.sum(jnp.where(live_rows, 0.0, grad_decoder_in), axis=0)
    grad_encoded = jnp.where(live_rows, grad_decoder_in, 0.0)
    grad_encoded, dec_early.state = pin(grad_encoded, dec_early.state)
    dec_early.fold()
    grad_encoded, dec_early.state = pin(grad_encoded, dec_early.state)

    grad_hidden, grad_fc1, grad_fc2 = feed_backward(grad_encoded, enc_feed, enc_fc2_whole)
    grad_hidden, grad_fc1, grad_fc2, dec_late.state, ends = pin(
        grad_hidden, grad_fc1, grad_fc2, dec_late.state, ends
    )
    dec_early.near()
    ends = ends + swap(ends, 4, devices)
    enc_late = scatter_late(grad_fc1, grad_fc2)
    grad_middle, grad_attended, grad_proj, enc_gain2_grad, enc_bias2_grad = middle_backward(
        grad_encoded, grad_hidden, enc_feed, enc_attended, vectors[2], vectors[3], enc_fc1_whole, enc_proj_whole
    )
    grad_attended, grad_proj, enc_late.state = pin(grad_attended, grad_proj, enc_late.state)
    enc_late.fold()
    grad_attended, enc_late.state, dec_early.state, ends = pin(grad_attended, enc_late.state, dec_early.state, ends)
    enc_late.near()
    ends = ends + swap(ends, 8, devices)
    dec_late.far()
    grad_projected = attend_backward(grad_attended, enc_projected, enc_log, live_keys, images)
    grad_qkv = narrow(outer_sum(enc_normed, grad_projected))
    grad_residual, enc_gain1_grad, enc_bias1_grad = inner_backward(
        grad_middle, grad_projected, residual, vectors[0], vectors[1], enc_qkv_whole
    )
    grad_small = [enc_gain1_grad, enc_bias1_grad, enc_gain2_grad, enc_bias2_grad]
    grad_small += [dec_gain1_grad, dec_bias1_grad, dec_gain2_grad, dec_bias2_grad, grad_mask]
    small_count = len(grad_small)
    grad_small = jnp.stack(grad_small).T
    grad_small = jnp.pad(grad_small, ((0, 0), (0, model_width - small_count)))
    grad_residual, grad_qkv, grad_small, dec_late.state, ends = pin(
        grad_residual, grad_qkv, grad_small, dec_late.state, ends
    )
    enc_early = scatter_early(grad_qkv, grad_proj, grad_small)
    rest = 16
    while rest < devices:
        ends = ends + swap(ends, rest, devices)
        rest *= 2
    enc_early.state, enc_late.state = pin(enc_early.state, enc_late.state)
    enc_early.fold()
    enc_early.state, enc_late.state = pin(enc_early.state, enc_late.state)
    enc_early.near()
    dec_late.along_upper()
    dec_late.state, enc_early.state = pin(dec_late.state, enc_early.state)
    enc_late.far()
    dec_early.far()
    enc_late.state, dec_early.state = pin(enc_late.state, dec_early.state)
    enc_late.along_upper()
    enc_early.far()
    enc_late.state, enc_early.state = pin(enc_late.state, enc_early.state)
    enc_early.along_upper()
    dec_early.along_upper()

    def block_sums(early, late):
        early, late = early.result(), late.result()
        return [from_units(early[:3]), early[3], from_units(late[:fc_count]), late[fc_count:].reshape(-1, model_width)]

    dec_big = block_sums(dec_early, dec_late)
    enc_big = block_sums(enc_early, enc_late)
    me = lax.axis_index("dp")
    inner_rows = diff_out.shape[0]
    loss_sum = ends[2 * CH, 0]
    ends = lax.dynamic_slice_in_dim(ends[: 2 * CH], me * inner_rows, inner_rows, axis=1)
    summed = list(enc_early.result()[4][:, :small_count].T)
    enc_summed = (summed[0], summed[1], enc_big[0], enc_big[1], summed[2], summed[3], enc_big[2], enc_big[3])
    dec_summed = (summed[4], summed[5], dec_big[0], dec_big[1], summed[6], summed[7], dec_big[2], dec_big[3], summed[8])
    diff_summed = (
        ends[:CH],
        mixed[shard_rows:],
        columns_sum(0, 1),
        mixed[:shard_rows],
        columns_sum(3, 6),
        columns_sum(1, 2),
        columns_sum(2, 3),
        columns_sum(6, 8),
        ends[CH:].T,
    )
    loss_mean = loss_sum / count_all
    grad_tokens = grad_residual.reshape(images, positions, model_width)
    return (
        loss_mean,
        grad_tokens,
        enc_summed[0],
        enc_summed[1],
        enc_summed[2],
        enc_summed[3],
        enc_summed[4],
        enc_summed[5],
        enc_summed[6],
        enc_summed[7],
        dec_summed[0],
        dec_summed[1],
        dec_summed[2],
        dec_summed[3],
        dec_summed[4],
        dec_summed[5],
        dec_summed[6],
        dec_summed[7],
        dec_summed[8],
        diff_summed[0],
        diff_summed[1],
        diff_summed[2],
        diff_summed[3],
        diff_summed[4],
        diff_summed[5],
        diff_summed[6],
        diff_summed[7],
        diff_summed[8],
    )


def solution(mesh):
    placed = (
        P("dp", None, None),
        P("dp", None, None),
        P("dp", None),
        P("dp"),
        P("dp", None),
        P("dp", None, None),
        P("dp"),
        P("dp"),
        P("dp", None),
        P("dp", None),
        P("dp"),
        P("dp"),
        P("dp", None),
        P("dp", None),
        P("dp"),
        P("dp"),
        P("dp", None),
        P("dp", None),
        P("dp"),
        P("dp"),
        P("dp", None),
        P("dp", None),
        P("dp"),
        P(None, "dp"),
        P("dp", None),
        P("dp", None),
        P("dp", None),
        P("dp", None),
        P("dp", None),
        P("dp", None),
        P("dp", None),
        P("dp", None),
    )
    return jax.shard_map(
        on_device,
        mesh=mesh,
        in_specs=placed,
        out_specs=(
            P(),
            P("dp", None, None),
            P("dp"),
            P("dp"),
            P("dp", None),
            P("dp", None),
            P("dp"),
            P("dp"),
            P("dp", None),
            P("dp", None),
            P("dp"),
            P("dp"),
            P("dp", None),
            P("dp", None),
            P("dp"),
            P("dp"),
            P("dp", None),
            P("dp", None),
            P("dp"),
            P(None, "dp"),
            P("dp", None),
            P("dp", None),
            P("dp", None),
            P("dp", None),
            P("dp", None),
            P("dp", None),
            P("dp", None),
            P("dp", None),
        ),
        check_vma=False,
    )
```

```python
import functools
import math

import jax
import jax.numpy as jnp
from jax import lax
from jax.experimental import pallas as pl
from jax.experimental.pallas import tpu as pltpu
from jax.sharding import PartitionSpec as P

HEAD = 64
CH = 16
BUF = 64
L = 256


def split_masks(devices):
    bits = devices.bit_length() - 2
    upper = min(2, bits - 2)
    first = (bits - upper) // 2
    second = bits - upper - first
    group = lambda low, count: [m << low for m in range(1 << count)]
    return group(1, first), group(1 + first, second), group(1 + first + second, upper)


def swap(block, mask, devices):
    return lax.ppermute(block, "dp", [(i, i ^ mask) for i in range(devices)])


def wide(part):
    return part.astype(jnp.float32)


def narrow(part):
    return part.astype(jnp.bfloat16)


def place_kernel(layout, kinds, *refs):
    pieces = refs[: len(layout)]
    outs = refs[len(layout) : len(layout) + len(kinds)]
    sems = refs[-1]
    me = lax.axis_index("dp")
    unit = pieces[0].shape[-1]
    copies = []
    for piece, masks in zip(pieces, layout):
        for spot, mask in enumerate(masks):
            base = 0
            for out, (count, side) in zip(outs, kinds):
                for j in range(count):
                    target = out.at[me ^ mask, j]
                    if side == "columns":
                        target = out.at[me ^ mask, :, pl.ds(j * unit, unit)]
                    copies.append(
                        pltpu.make_async_copy(piece.at[spot, base + j], target, sems.at[len(copies)])
                    )
                base += count
    for copy in copies:
        copy.start()
    for copy in copies:
        copy.wait()


def whole_shape(kind, rows, unit):
    count, side = kind
    return (rows, count * unit) if side == "columns" else (count, rows, unit)


def place(pieces, layout, kinds, devices):
    _, units, rows, unit = pieces[0].shape
    dtype = pieces[0].dtype
    moved = 2 * devices * units * rows * unit * dtype.itemsize
    return pl.pallas_call(
        functools.partial(place_kernel, layout, kinds),
        out_shape=[jax.ShapeDtypeStruct((devices,) + whole_shape(kind, rows, unit), dtype) for kind in kinds],
        in_specs=[pl.BlockSpec(memory_space=pl.ANY)] * len(pieces),
        out_specs=[pl.BlockSpec(memory_space=pltpu.VMEM)] * len(kinds),
        scratch_shapes=[pltpu.SemaphoreType.DMA((devices * units,))],
        compiler_params=pltpu.CompilerParams(vmem_limit_bytes=24 << 20),
        cost_estimate=pl.CostEstimate(flops=0, bytes_accessed=moved, transcendentals=0),
    )(*pieces)


def pin(*trees):
    return lax.optimization_barrier(trees)


class Gather:
    def __init__(self, own, kinds, devices):
        self.kinds, self.devices = kinds, devices
        self.first, self.second, self.upper = split_masks(devices)
        self.state = [own]

    def along_upper(self):
        (own,) = self.state
        held = [own] + [swap(own, m, self.devices) for m in self.upper[1:]]
        self.state = [jnp.stack(held[:2]), jnp.stack(held[2:])]

    def beside(self):
        (own,) = self.state
        self.state = [own, swap(own, self.upper[1], self.devices)]

    def beyond(self):
        pair = jnp.stack(self.state)
        self.state = [pair, swap(pair, self.upper[2], self.devices)]

    def near(self):
        self.layout, held, self.state = [], self.state, []
        for block, base, masks in zip(held, (self.upper[:2], self.upper[2:]), (self.first, self.second)):
            self.state.append([block if m == 0 else swap(block, m, self.devices) for m in masks])
            self.layout.append([m ^ v for m in masks for v in base])

    def far(self):
        self.state = [jnp.concatenate(blocks, axis=0) for blocks in self.state]
        for block, base, masks in zip(self.state[:2], self.layout[:2], (self.second, self.first)):
            for m in masks[1:]:
                self.state.append(swap(block, m, self.devices))
                self.layout.append([m ^ v for v in base])
        self.across(0, 2)

    def across(self, start, stop):
        self.state += [swap(block, 1, self.devices) for block in self.state[start:stop]]
        self.layout += [[1 ^ v for v in base] for base in self.layout[start:stop]]

    def last(self):
        self.across(2, len(self.state) - 2)

    def whole(self):
        return place(self.state, self.layout, self.kinds, self.devices)


def as_units(shard, unit):
    rows, width = shard.shape
    return shard.reshape(rows, width // unit, unit).transpose(1, 0, 2)


def fold_kernel(sizes, kinds, table, *refs):
    count = len(kinds)
    mine, theirs, outs = refs[:count], refs[count : 2 * count], refs[2 * count :]
    step = pl.program_id(0)
    start = 0
    for out, size in zip(outs, sizes):
        unit = out.shape[-1]

        @pl.when((step >= start) & (step < start + size))
        def _(out=out, unit=unit):
            base = 0
            for own, other, (units, side) in zip(mine, theirs, kinds):
                for j in range(units):
                    spot = (0, j) if side == "rows" else (0, slice(None), slice(j * unit, (j + 1) * unit))
                    out[0, base + j] = narrow(wide(own[spot]) + wide(other[spot]))
                base += units

        start += size


def fold(mine, theirs, kinds, slots, devices):
    unit = theirs[0].shape[-1] // (kinds[0][0] if kinds[0][1] == "columns" else 1)
    rows = theirs[0].shape[-2]
    units = sum(count for count, _ in kinds)
    sizes = [len(group) for group in slots]
    me = lax.axis_index("dp")
    order = jnp.asarray([chip for group in slots for chip in group], jnp.int32)
    table = (me // 2) ^ order
    table = jnp.concatenate([table, (me % 2).reshape(1).astype(jnp.int32)])
    total = len(order)
    zeros = lambda array: (0,) * (array.ndim - 1)
    own_spec = lambda a: pl.BlockSpec((1,) + a.shape[1:], lambda s, t, z=zeros(a): (t[s] * 2 + t[total],) + z)
    other_spec = lambda a: pl.BlockSpec((1,) + a.shape[1:], lambda s, t, z=zeros(a): (t[s],) + z)
    out_specs, start = [], 0
    for size in sizes:
        out_specs.append(
            pl.BlockSpec(
                (1, units, rows, unit), lambda s, t, lo=start, top=size - 1: (jnp.clip(s - lo, 0, top), 0, 0, 0)
            )
        )
        start += size
    moved = 3 * total * units * rows * unit * 2
    return pl.pallas_call(
        functools.partial(fold_kernel, sizes, kinds),
        out_shape=[jax.ShapeDtypeStruct((size, units, rows, unit), jnp.bfloat16) for size in sizes],
        grid_spec=pltpu.PrefetchScalarGridSpec(
            num_scalar_prefetch=1,
            grid=(total,),
            in_specs=[own_spec(a) for a in mine] + [other_spec(a) for a in theirs],
            out_specs=out_specs,
        ),
        compiler_params=pltpu.CompilerParams(
            dimension_semantics=("arbitrary",), vmem_limit_bytes=32 << 20
        ),
        cost_estimate=pl.CostEstimate(flops=moved, bytes_accessed=moved, transcendentals=0),
    )(table, *mine, *theirs)


class Scatter:
    def __init__(self, wholes, kinds, devices):
        self.kinds, self.devices, self.wholes = kinds, devices, wholes
        first, second, upper = ([m // 2 for m in masks] for masks in split_masks(devices))
        half = len(upper) // 2
        self.upper = upper
        self.routes = ((upper[:half], second, first), (upper[half:], first, second))
        core = lax.axis_index("dp") % 2
        self.state = []
        for whole in wholes:
            pairs = whole.reshape((devices // 2, 2) + whole.shape[1:])
            self.state.append(swap(lax.dynamic_index_in_dim(pairs, 1 - core, 1, keepdims=False), 1, devices))

    def fold(self):
        slots = [[u ^ n ^ f for f in far for u in ups] for ups, near, far in self.routes for n in near]
        self.state = fold(self.wholes, self.state, self.kinds, slots, self.devices)
        self.wholes = None

    def near(self):
        masks = [n for _, near, _ in self.routes for n in near]
        self.state = [g if n == 0 else swap(g, 2 * n, self.devices) for g, n in zip(self.state, masks)]

    def far(self):
        held, self.state = self.state, []
        for ups, near, far in self.routes:
            groups, held = held[: len(near)], held[len(near) :]
            blocks = [wide(g).reshape((len(far), len(ups)) + g.shape[1:]) for g in groups]
            for spot, f in enumerate(far):
                total = blocks[0][spot]
                for block in blocks[1:]:
                    total = total + block[spot]
                total = narrow(total)
                self.state.append(total if f == 0 else swap(total, 2 * f, self.devices))

    def along_upper(self):
        held, parts = self.state, []
        for ups, near, far in self.routes:
            groups, held = held[: len(far)], held[len(far) :]
            for spot in range(len(ups)):
                total = wide(groups[0][spot])
                for g in groups[1:]:
                    total = total + wide(g[spot])
                parts.append(narrow(total))
        self.state = [p if u == 0 else swap(p, 2 * u, self.devices) for p, u in zip(parts, self.upper)]

    def result(self):
        total = wide(self.state[0])
        for part in self.state[1:]:
            total = total + wide(part)
        return total


def from_units(units):
    count, rows, unit = units.shape
    return units.transpose(1, 0, 2).reshape(rows, count * unit)


def sum_all(block, devices):
    mask = 1
    while mask < devices:
        block = block + swap(block, mask, devices)
        mask *= 2
    return block


def in_three(values):
    first = lax.reduce_precision(values, 8, 7)
    second = lax.reduce_precision(values - first, 8, 7)
    third = values - first - second
    return [narrow(part) for part in (first, second, third)]


def layer_norm(residual, gain, offset):
    centred = residual - jnp.mean(residual, axis=-1, keepdims=True)
    spread = jnp.mean(centred * centred, axis=-1, keepdims=True)
    return centred * lax.rsqrt(spread + 1e-06) * gain + offset


def plain_norm(residual):
    centred = residual - jnp.mean(residual, axis=-1, keepdims=True)
    spread = jnp.mean(centred * centred, axis=-1, keepdims=True)
    return centred * lax.rsqrt(spread + 1e-06)


def modulate(residual, shift_part, scale_part):
    return plain_norm(residual) * (1.0 + scale_part) + shift_part


def exact_gelu(hidden):
    below = 0.5 + 0.5 * lax.erf(hidden * math.sqrt(0.5))
    density = jnp.exp(-0.5 * hidden * hidden) * (1.0 / math.sqrt(2.0 * math.pi))
    return hidden * below, below + hidden * density


def matmul(left, right):
    return jnp.dot(left, right, preferred_element_type=jnp.float32)


def outer_sum(left, right):
    return lax.dot_general(
        left, right, (((0,), (0,)), ((), ())), preferred_element_type=jnp.float32
    )


def times_transpose(left, right):
    return lax.dot_general(
        left, right, (((1,), (1,)), ((), ())), preferred_element_type=jnp.float32
    )


def attention_scores(query_rows, key_rows, keys_live):
    scores = jnp.einsum(
        "bqhe,bkhe->bhqk", query_rows, key_rows, preferred_element_type=jnp.float32
    ) * HEAD ** (-0.5)
    return jnp.where(keys_live[:, None, None, :], scores, -1e30)


def split_heads(projected, images):
    positions = projected.shape[0] // images
    head_count = projected.shape[1] // (3 * HEAD)
    shaped = projected.reshape(images, positions, 3, head_count, HEAD)
    return (shaped[:, :, 0], shaped[:, :, 1], shaped[:, :, 2])


def project_in(residual, gain, offset, qkv_w):
    normed = narrow(layer_norm(residual, wide(gain), wide(offset)))
    return normed, narrow(matmul(normed, qkv_w))


def attend_forward(projected, keys_live, images):
    query_rows, key_rows, value_rows = split_heads(projected, images)
    scores = attention_scores(query_rows, key_rows, keys_live)
    row_peak = jnp.max(scores, axis=-1, keepdims=True)
    log_total = row_peak + jnp.log(jnp.sum(jnp.exp(scores - row_peak), axis=-1, keepdims=True))
    soft_rounded = narrow(jnp.exp(scores - log_total))
    attended = jnp.einsum("bhqk,bkhe->bqhe", soft_rounded, value_rows, preferred_element_type=jnp.float32)
    return log_total, narrow(attended).reshape(projected.shape[0], -1)


def feed_in(residual, attended, proj_w, gain, offset, fc1_w):
    middle = residual + matmul(attended, proj_w)
    normed = narrow(layer_norm(middle, wide(gain), wide(offset)))
    active, slope = exact_gelu(matmul(normed, fc1_w))
    return middle, normed, slope, narrow(active)


def feed_backward(grad_output, saved, fc2_w):
    _, normed, slope, active = saved
    grad_branch = narrow(grad_output)
    grad_active = times_transpose(grad_branch, fc2_w)
    grad_hidden = narrow(grad_active * slope)
    return grad_hidden, narrow(outer_sum(normed, grad_hidden)), narrow(outer_sum(active, grad_branch))


def middle_backward(grad_output, grad_hidden, saved, attended, gain, offset, fc1_w, proj_w):
    grad_normed = times_transpose(grad_hidden, fc1_w)
    back = jax.vjp(layer_norm, saved[0], wide(gain), wide(offset))[1]
    grad_norm, grad_gain, grad_offset = back(grad_normed)
    grad_middle = grad_output + grad_norm
    grad_attention = narrow(grad_middle)
    grad_proj = narrow(outer_sum(attended, grad_attention))
    grad_attended = narrow(times_transpose(grad_attention, proj_w))
    return grad_middle, grad_attended, grad_proj, grad_gain, grad_offset


def attend_backward(grad_attended, projected, log_total, keys_live, images):
    rows, model_width = grad_attended.shape
    grad_attended = grad_attended.reshape(images, rows // images, model_width // HEAD, HEAD)
    query_rows, key_rows, value_rows = split_heads(projected, images)
    scores = attention_scores(query_rows, key_rows, keys_live)
    soft_full = jnp.exp(scores - log_total)
    soft_rounded = narrow(soft_full)
    grad_value = jnp.einsum("bhqk,bqhe->bkhe", soft_rounded, grad_attended, preferred_element_type=jnp.float32)
    grad_soft = jnp.einsum("bqhe,bkhe->bhqk", grad_attended, value_rows, preferred_element_type=jnp.float32)
    grad_scores = soft_full * (grad_soft - jnp.sum(grad_soft * soft_full, axis=-1, keepdims=True))
    grad_scores = narrow(grad_scores)
    grad_query = jnp.einsum(
        "bhqk,bkhe->bqhe", grad_scores, key_rows, preferred_element_type=jnp.float32
    ) * HEAD ** (-0.5)
    grad_key = jnp.einsum(
        "bhqk,bqhe->bkhe", grad_scores, query_rows, preferred_element_type=jnp.float32
    ) * HEAD ** (-0.5)
    grad_projected = narrow(jnp.stack([grad_query, grad_key, grad_value], axis=2))
    return grad_projected.reshape(rows, 3 * model_width)


def inner_backward(grad_middle, grad_projected, residual, gain, offset, qkv_w):
    grad_normed = times_transpose(grad_projected, qkv_w)
    back = jax.vjp(layer_norm, residual, wide(gain), wide(offset))[1]
    grad_norm, grad_gain, grad_offset = back(grad_normed)
    return grad_middle + grad_norm, grad_gain, grad_offset


def silu_slope(value):
    gate = jax.nn.sigmoid(value)
    return gate * (1.0 + value * (1.0 - gate))


def normed_rows(value):
    centred = value - jnp.mean(value, axis=-1, keepdims=True)
    inverse = lax.rsqrt(jnp.mean(centred * centred, axis=-1, keepdims=True) + 1e-06)
    return centred * inverse, inverse


def norm_back(grad, normed, inverse):
    spread = jnp.mean(grad * normed, axis=-1, keepdims=True)
    return inverse * (grad - jnp.mean(grad, axis=-1, keepdims=True) - normed * spread)


def head_kernel(
    noisy, noise, sinusoid, live, cond, in_w, time1_w, time2_w, cond_w, wide_w, mlp_w, out_w,
    lefts, rights, grad_time_pre, final_in, grad_output, grad_start, grad_cond_emb, grad_cond, loss,
    time_pre, context_pre, start, first_pre, branch, middle, product, modulation, total,
):
    step = pl.program_id(0)
    rows, width = time_pre.shape
    part = lambda array, i, count=1: array.at[:, i * width : (i + count) * width]

    def by_rows(body):
        body(pl.ds(0, rows))

    def columns(i):
        return slice(i * width, (i + 1) * width)

    time_pre[...] = matmul(sinusoid[...], time1_w[...])

    def time_rows(r):
        lefts[r, columns(0)] = narrow(jax.nn.silu(time_pre[r, :]))

    by_rows(time_rows)
    context_pre[...] = matmul(part(lefts, 0)[...], time2_w[...]) + matmul(cond[...], cond_w[...])

    def context_rows(r):
        lefts[r, columns(3)] = narrow(jax.nn.silu(context_pre[r, :]))

    by_rows(context_rows)
    for i in range(5):
        part(modulation, i)[...] = matmul(part(lefts, 3)[...], part(wide_w, i)[...])
    start[...] = matmul(noisy[...], in_w[...])

    def first_rows(r):
        normed, _ = normed_rows(start[r, :])
        lefts[r, columns(1)] = narrow(normed * (1.0 + modulation[r, columns(1)]) + modulation[r, columns(0)])

    by_rows(first_rows)
    first_pre[...] = matmul(part(lefts, 1)[...], part(mlp_w, 0)[...])

    def active_rows(r):
        lefts[r, columns(2)] = narrow(jax.nn.silu(first_pre[r, :]))

    by_rows(active_rows)
    branch[...] = matmul(part(lefts, 2)[...], part(mlp_w, 1)[...])

    def middle_rows(r):
        value = start[r, :] + modulation[r, columns(2)] * branch[r, :]
        middle[r, :] = value
        normed, _ = normed_rows(value)
        final_in[r, :] = narrow(normed * (1.0 + modulation[r, columns(4)]) + modulation[r, columns(3)])

    by_rows(middle_rows)
    residue = times_transpose(final_in[...], out_w[...]) - noise[...]
    scale = 1.0 / (pl.num_programs(0) * residue.shape[1])
    weighted = live[...] * residue
    grad_output[...] = narrow(2.0 * weighted * scale)

    @pl.when(step == 0)
    def _():
        loss[...] = jnp.zeros_like(loss)
        total[...] = jnp.zeros_like(total)

    loss[...] += jnp.sum(weighted * residue) * scale
    product[...] = matmul(grad_output[...], out_w[...])

    def middle_back(r):
        grad = product[r, :]
        normed, inverse = normed_rows(middle[r, :])
        rights[r, columns(6)] = narrow(grad)
        rights[r, columns(7)] = narrow(grad * normed)
        grad_middle = norm_back(grad * (1.0 + modulation[r, columns(4)]), normed, inverse)
        middle[r, :] = grad_middle
        rights[r, columns(2)] = narrow(modulation[r, columns(2)] * grad_middle)
        rights[r, columns(5)] = narrow(branch[r, :] * grad_middle)

    by_rows(middle_back)
    product[...] = times_transpose(part(rights, 2)[...], part(mlp_w, 1)[...])

    def active_back(r):
        rights[r, columns(1)] = narrow(product[r, :] * silu_slope(first_pre[r, :]))

    by_rows(active_back)
    product[...] = times_transpose(part(rights, 1)[...], part(mlp_w, 0)[...])

    def first_back(r):
        grad = product[r, :]
        normed, inverse = normed_rows(start[r, :])
        rights[r, columns(3)] = narrow(grad)
        rights[r, columns(4)] = narrow(grad * normed)
        back = norm_back(grad * (1.0 + modulation[r, columns(1)]), normed, inverse)
        grad_start[r, :] = narrow(middle[r, :] + back)

    by_rows(first_back)
    product[...] = times_transpose(part(rights, 3)[...], part(wide_w, 0)[...])
    for i in range(1, 5):
        product[...] += times_transpose(part(rights, 3 + i)[...], part(wide_w, i)[...])

    def context_back(r):
        grad = product[r, :] * silu_slope(context_pre[r, :])
        rights[r, columns(0)] = narrow(grad)
        total[r, :] += grad

    by_rows(context_back)
    product[...] = times_transpose(part(rights, 0)[...], time2_w[...])

    def time_back(r):
        grad_time_pre[r, :] = narrow(product[r, :] * silu_slope(time_pre[r, :]))

    by_rows(time_back)

    @pl.when(step == pl.num_programs(0) - 1)
    def _():
        grad_cond_emb[...] = narrow(total[...])
        grad_cond[...] = narrow(times_transpose(grad_cond_emb[...], cond_w[...]))


def head_pass(noisy, noise, sinusoid, live, cond, weights):
    rows = cond.shape[0]
    flat_rows = noisy.shape[0]
    width = weights[0].shape[1]
    bf16, f32 = jnp.bfloat16, jnp.float32
    by_copy = lambda columns: pl.BlockSpec((rows, columns), lambda e: (e, 0))
    whole = lambda array: pl.BlockSpec(array.shape, lambda e: (0, 0))
    resident = pl.BlockSpec(memory_space=pltpu.VMEM)
    outs = [(flat_rows, 4 * width), (flat_rows, 8 * width), (flat_rows, width), (flat_rows, width)]
    outs += [(flat_rows, CH), (flat_rows, width), (rows, width), cond.shape]
    outs = [jax.ShapeDtypeStruct(shape, bf16) for shape in outs] + [jax.ShapeDtypeStruct((8, 128), f32)]
    out_specs = [by_copy(out.shape[1]) for out in outs[:6]] + [whole(out) for out in outs[6:]]
    flops = 6 * flat_rows * sum(weight.size for weight in weights)
    return pl.pallas_call(
        head_kernel,
        out_shape=outs,
        grid=(flat_rows // rows,),
        in_specs=[by_copy(noisy.shape[1]), by_copy(noise.shape[1]), by_copy(sinusoid.shape[1]), whole(live), whole(cond)]
        + [resident] * len(weights),
        out_specs=out_specs,
        scratch_shapes=[pltpu.VMEM((rows, width), f32)] * 7
        + [pltpu.VMEM((rows, 5 * width), f32), pltpu.VMEM((rows, width), f32)],
        compiler_params=pltpu.CompilerParams(dimension_semantics=("arbitrary",), vmem_limit_bytes=60 << 20),
        cost_estimate=pl.CostEstimate(flops=flops, bytes_accessed=60 << 20, transcendentals=flat_rows * width * 8),
    )(noisy, noise, sinusoid, live, cond, *weights)


def products_kernel(lefts, rights, mixed, out):
    unit = pl.program_id(0)

    @pl.when(unit < pl.num_programs(0) - 1)
    def _():
        size = 256

        def visit(i, carry):
            r = pl.ds(pl.multiple_of(i * size, size), size)
            out[r, :] = narrow(outer_sum(lefts[:, r], rights[...]))
            return carry

        lax.fori_loop(0, out.shape[0] // size, visit, 0, unroll=True)

    @pl.when(unit == pl.num_programs(0) - 1)
    def _():
        out[...] = mixed[...]


def products(lefts, rights, mixed):
    flat_rows = lefts.shape[0]
    width = mixed.shape[1]
    last_left, last_right = lefts.shape[1] // width - 1, rights.shape[1] // width - 1
    units = last_right + 2
    return pl.pallas_call(
        products_kernel,
        out_shape=jax.ShapeDtypeStruct((width, units * width), jnp.bfloat16),
        grid=(units,),
        in_specs=[
            pl.BlockSpec((flat_rows, width), lambda u: (0, jnp.minimum(u, last_left))),
            pl.BlockSpec((flat_rows, width), lambda u: (0, jnp.minimum(u, last_right))),
            pl.BlockSpec(memory_space=pltpu.VMEM),
        ],
        out_specs=pl.BlockSpec((width, width), lambda u: (0, u)),
        compiler_params=pltpu.CompilerParams(dimension_semantics=("arbitrary",), vmem_limit_bytes=40 << 20),
        cost_estimate=pl.CostEstimate(
            flops=2 * (units - 1) * flat_rows * width * width, bytes_accessed=60 << 20, transcendentals=0
        ),
    )(lefts, rights, mixed)


def head_inputs(target_rows, step_rows, noise_rows, half_freq):
    flat_rows = step_rows.size
    steps_float = step_rows.astype(jnp.float32)
    angle_noise = (steps_float / 1000.0 + 0.008) / 1.008 * (math.pi / 2)
    keep_part = jnp.cos(angle_noise) ** 2
    noisy_rows = (
        jnp.sqrt(keep_part)[:, :, None] * target_rows[None, :, :]
        + jnp.sqrt(1.0 - keep_part)[:, :, None] * noise_rows
    )
    frequency = jnp.exp(-math.log(10000.0) * jnp.arange(half_freq, dtype=jnp.float32) / half_freq)
    phases = steps_float.reshape(flat_rows, 1) * frequency[None, :]
    sinusoid = narrow(jnp.concatenate([jnp.cos(phases), jnp.sin(phases)], axis=1))
    return narrow(noisy_rows.reshape(flat_rows, CH)), sinusoid


def on_device(
    tokens,
    latents,
    orders,
    counts,
    timesteps,
    noise,
    enc_gain1,
    enc_bias1,
    enc_qkv,
    enc_proj,
    enc_gain2,
    enc_bias2,
    enc_fc1,
    enc_fc2,
    dec_gain1,
    dec_bias1,
    dec_qkv,
    dec_proj,
    dec_gain2,
    dec_bias2,
    dec_fc1,
    dec_fc2,
    mask_token,
    diff_in,
    diff_time1,
    diff_time2,
    diff_cond,
    diff_ada,
    diff_mlp1,
    diff_mlp2,
    diff_final,
    diff_out,
):
    devices = lax.axis_size("dp")
    images = tokens.shape[0]
    positions = tokens.shape[1]
    model_width = tokens.shape[2]
    tokens_here = images * L
    shard_rows = enc_proj.shape[0]
    flat_latents = latents.reshape(tokens_here, CH)
    sums_here = jnp.sum(flat_latents, axis=0)
    squares_here = jnp.sum(flat_latents * flat_latents, axis=0)
    count_here = jnp.sum(counts).astype(jnp.float32)
    statistics = jnp.concatenate([sums_here, squares_here, count_here[None]])
    vectors = [enc_gain1, enc_bias1, enc_gain2, enc_bias2, dec_gain1, dec_bias1, dec_gain2, dec_bias2, mask_token]
    statistics = jnp.concatenate(in_three(statistics))[None]
    statistics = jnp.pad(statistics, ((0, 0), (0, 512 - statistics.shape[1])))
    ends = jnp.concatenate([diff_in.T, diff_out], axis=1).reshape(2, -1)
    ends_width = ends.shape[1]
    ends = jnp.pad(ends, ((0, 0), (0, 512 - ends_width)))
    packed = jnp.concatenate([statistics, ends], axis=0)
    packed = jnp.concatenate(
        [
            jnp.pad(jnp.stack(vectors, axis=1), ((0, 0), (0, 128 - len(vectors)))),
            jnp.pad(packed, ((0, shard_rows - 3), (0, model_width - 128 - 512))),
        ],
        axis=1,
    )[None]

    inner_width = diff_mlp1.shape[1]
    def feed_shard(fc1, fc2):
        return jnp.concatenate([fc1] + list(fc2.reshape(-1, shard_rows, model_width)), axis=1)

    mlp_shard = jnp.concatenate([diff_mlp1, diff_mlp2], axis=1)
    spare_rows = mlp_shard.shape[0] - shard_rows
    spare_shard = mlp_shard[shard_rows:].reshape(2 * spare_rows, -1)
    spare_shard = jnp.pad(spare_shard, ((0, shard_rows - 2 * spare_rows), (0, 0)))
    feed_shards = [feed_shard(enc_fc1, enc_fc2), feed_shard(dec_fc1, dec_fc2), mlp_shard[:shard_rows], spare_shard]
    time_units = jnp.stack([diff_time2, jnp.concatenate([diff_cond, diff_time1], axis=0)])
    wide_units = jnp.concatenate([as_units(diff_ada, inner_width), as_units(diff_final, inner_width)], axis=0)

    qkv_kinds, proj_kinds = ((3, "columns"),), ((1, "columns"),)
    fc_count = enc_fc1.shape[1] // model_width
    late_kinds = proj_kinds + ((fc_count, "columns"), (fc_count, "rows"))

    def early_units(qkv, proj, extra):
        return jnp.concatenate([as_units(qkv, model_width), proj[None]] + extra, axis=0)

    enc_early = Gather(early_units(enc_qkv, enc_proj, [packed]), qkv_kinds + proj_kinds + proj_kinds, devices)
    dec_early = Gather(early_units(dec_qkv, dec_proj, []), qkv_kinds + proj_kinds, devices)
    head_time = Gather(time_units, ((1, "columns"),) * 2, devices)
    head_wide = Gather(wide_units, ((5, "columns"),), devices)

    gathered = lax.all_gather(jnp.concatenate(feed_shards, axis=1), "dp", axis=0, tiled=True)
    enc_early.along_upper()
    enc_early.state, dec_early.state = pin(enc_early.state, dec_early.state)
    enc_early.near()
    dec_early.beside()
    enc_early.state, dec_early.state = pin(enc_early.state, dec_early.state)
    enc_early.far()
    dec_early.beyond()
    enc_early.state, dec_early.state, head_time.state = pin(enc_early.state, dec_early.state, head_time.state)
    enc_early.last()
    dec_early.near()
    head_time.beside()
    enc_early.state, dec_early.state, head_time.state = pin(enc_early.state, dec_early.state, head_time.state)
    dec_early.far()
    head_time.beyond()
    enc_qkv_whole, enc_proj_whole, small_full = enc_early.whole()
    enc_qkv_whole, enc_proj_whole = (part.reshape(model_width, -1) for part in (enc_qkv_whole, enc_proj_whole))

    vectors = list(wide(small_full.reshape(model_width, -1)[:, :16].T))
    ends = small_full.reshape(devices, shard_rows, -1)[:, 1:3, 128 : 128 + ends_width].reshape(-1, 2 * CH)
    in_full, out_full = ends[:, :CH].T, ends[:, CH:].T
    statistics = wide(small_full.reshape(devices, shard_rows, -1)[:, 0, 128 : 128 + 3 * (2 * CH + 1)])
    statistics = jnp.sum(jnp.sum(statistics.reshape(devices, 3, -1), axis=1), axis=0)
    sums_all, squares_all, count_all = statistics[:CH], statistics[CH : 2 * CH], statistics[2 * CH]
    cell_count = tokens_here * devices
    average = sums_all / cell_count
    spread = squares_all / cell_count - average * average
    target = ((flat_latents - average) * lax.rsqrt(spread + 1e-06)).astype(jnp.bfloat16)

    masked = (orders < counts[:, None]).astype(jnp.int32)
    flag_rows = masked.reshape(tokens_here)
    rank_rows = jnp.cumsum(flag_rows) - flag_rows
    slot_count = -(-tokens_here // devices)
    copies = timesteps.shape[1]
    drawn = jnp.concatenate(
        [noise.reshape(devices, slot_count, -1), timesteps.astype(jnp.float32).reshape(devices, slot_count, -1)], axis=2
    )
    drawn = lax.all_to_all(drawn, "dp", split_axis=0, concat_axis=0, tiled=True)
    drawn = drawn.reshape(devices * slot_count, -1)
    slots = jnp.arange(devices * slot_count, dtype=jnp.int32)
    ranks = slots % slot_count * devices + slots // slot_count
    chooser = (ranks[None, :] == rank_rows[:, None]) & (flag_rows[:, None] > 0)
    drawn = jnp.dot(
        chooser.astype(jnp.float32), drawn, precision=lax.Precision.HIGHEST, preferred_element_type=jnp.float32
    )
    noise_rows = drawn[:, : copies * CH].reshape(tokens_here, copies, CH).transpose(1, 0, 2)
    step_rows = drawn[:, copies * CH :].T

    mask_vector = vectors[8].astype(jnp.float32)

    live_keys = jnp.concatenate([jnp.ones((images, BUF), jnp.int32), 1 - masked], axis=1) > 0
    all_live = jnp.ones((images, positions), jnp.bool_)
    live_rows = live_keys.reshape(images * positions, 1)
    residual = tokens.astype(jnp.float32).reshape(images * positions, model_width)
    enc_normed, enc_projected = project_in(residual, vectors[0], vectors[1], enc_qkv_whole)
    enc_projected, dec_early.state, head_time.state, head_wide.state = pin(
        enc_projected, dec_early.state, head_time.state, head_wide.state
    )
    dec_early.last()
    head_time.near()
    head_wide.beside()
    enc_log, enc_attended = attend_forward(enc_projected, live_keys, images)

    def feed_whole(first):
        unit = lambda i: gathered[:, (first + i) * model_width : (first + i + 1) * model_width]
        fc2 = [unit(fc_count + i).reshape(devices, shard_rows, -1) for i in range(fc_count)]
        fc2 = jnp.stack(fc2, axis=1)
        return gathered[:, first * model_width : (first + fc_count) * model_width], fc2.reshape(-1, model_width)

    enc_attended, dec_early.state, head_time.state, head_wide.state = pin(
        enc_attended, dec_early.state, head_time.state, head_wide.state
    )
    head_time.far()
    head_wide.beyond()
    dec_qkv_whole, dec_proj_whole = (whole.reshape(model_width, -1) for whole in dec_early.whole())
    enc_attended, dec_qkv_whole, dec_proj_whole = pin(enc_attended, dec_qkv_whole, dec_proj_whole)
    enc_fc1_whole, enc_fc2_whole = feed_whole(0)
    enc_feed = feed_in(residual, enc_attended, enc_proj_whole, vectors[2], vectors[3], enc_fc1_whole)
    enc_feed, dec_qkv_whole, dec_proj_whole, head_time.state, head_wide.state = pin(
        enc_feed, dec_qkv_whole, dec_proj_whole, head_time.state, head_wide.state
    )
    head_time.last()
    head_wide.near()
    encoded = enc_feed[0] + matmul(enc_feed[3], enc_fc2_whole)
    decoder_in = jnp.where(live_rows, encoded, mask_vector[None, :])
    dec_normed, dec_projected = project_in(decoder_in, vectors[4], vectors[5], dec_qkv_whole)
    dec_projected, head_time.state, head_wide.state = pin(dec_projected, head_time.state, head_wide.state)
    head_wide.far()
    dec_log, dec_attended = attend_forward(dec_projected, all_live, images)
    dec_attended, head_wide.state = pin(dec_attended, head_wide.state)
    head_wide.last()
    time2_full, mixed = (whole.reshape(-1, inner_width) for whole in head_time.whole())
    mixed = mixed.reshape(devices, -1, inner_width)
    cond_full = mixed[:, :shard_rows].reshape(-1, inner_width)
    time1_full = mixed[:, shard_rows:].reshape(-1, inner_width)
    noisy, sinusoid = head_inputs(wide(target), step_rows, noise_rows, time1_full.shape[0] // 2)
    live_column = wide(flag_rows)[:, None]
    noise_flat = noise_rows.reshape(-1, CH)
    dec_fc1_whole, dec_fc2_whole = feed_whole(2 * fc_count)
    dec_feed = feed_in(decoder_in, dec_attended, dec_proj_whole, vectors[6], vectors[7], dec_fc1_whole)
    dec_feed, in_full, out_full, cond_full, time1_full, time2_full, noisy, sinusoid = pin(
        dec_feed, in_full, out_full, cond_full, time1_full, time2_full, noisy, sinusoid
    )
    decoded = dec_feed[0] + matmul(dec_feed[3], dec_fc2_whole)
    cond_here = narrow(decoded.reshape(images, positions, model_width)[:, BUF:].reshape(tokens_here, model_width))
    wide_full = head_wide.whole()[0].reshape(-1, 5 * inner_width)
    mlp_parts = gathered[:, 4 * fc_count * model_width :].reshape(devices, shard_rows, -1)
    mlp_parts = [mlp_parts[:, :, : 2 * inner_width], mlp_parts[:, : 2 * spare_rows, 2 * inner_width :].reshape(devices, spare_rows, -1)]
    mlp_full = jnp.concatenate(mlp_parts, axis=1).reshape(inner_width, -1)
    lefts, rights, grad_time_pre, final_in, grad_output, grad_start, grad_cond_emb, grad_cond, loss_sum = head_pass(
        noisy,
        noise_flat,
        sinusoid,
        live_column,
        cond_here,
        (in_full, time1_full, time2_full, cond_full, wide_full, mlp_full, out_full),
    )
    ends = jnp.concatenate([outer_sum(noisy, grad_start), outer_sum(grad_output, final_in)], axis=0)
    loss_row = jnp.full((1, inner_width), loss_sum[0, 0], jnp.float32)
    ends = jnp.concatenate([ends, loss_row], axis=0)
    by_device = lambda part: narrow(part).reshape(devices, -1, part.shape[1])
    grad_time1, grad_cond_w = outer_sum(sinusoid, grad_time_pre), outer_sum(cond_here, grad_cond_emb)
    mixed = jnp.concatenate([by_device(grad_cond_w), by_device(grad_time1)], axis=1).reshape(-1, inner_width)
    grad_cond, diff_sum = pin(grad_cond, products(lefts, rights, mixed))
    diff_sum = lax.psum_scatter(diff_sum, "dp", scatter_dimension=0, tiled=True)
    columns_sum = lambda lo, hi: wide(diff_sum[:, lo * inner_width : hi * inner_width])
    mixed = columns_sum(8, 9)
    def scatter_late(fc1, fc2):
        fc1, fc2 = by_device(fc1), fc2.reshape(devices, -1, shard_rows, model_width)
        return Scatter([fc1, fc2], late_kinds[1:], devices)

    def scatter_early(*grads):
        return Scatter([by_device(grad) for grad in grads], qkv_kinds + proj_kinds * (len(grads) - 1), devices)

    grad_decoded = jnp.concatenate(
        [
            jnp.zeros((images, BUF, model_width), jnp.float32),
            grad_cond.astype(jnp.float32).reshape(images, L, model_width),
        ],
        axis=1,
    )
    grad_decoded = grad_decoded.reshape(images * positions, model_width)
    grad_hidden, grad_fc1, grad_fc2 = feed_backward(grad_decoded, dec_feed, dec_fc2_whole)
    grad_hidden, grad_fc1, grad_fc2, ends = pin(grad_hidden, grad_fc1, grad_fc2, ends)
    dec_late = scatter_late(grad_fc1, grad_fc2)
    ends = ends + swap(ends, 1, devices)
    grad_middle, grad_attended, grad_proj, dec_gain2_grad, dec_bias2_grad = middle_backward(
        grad_decoded, grad_hidden, dec_feed, dec_attended, vectors[6], vectors[7], dec_fc1_whole, dec_proj_whole
    )
    grad_attended, grad_proj, dec_late.state = pin(grad_attended, grad_proj, dec_late.state)
    dec_late.fold()
    grad_attended, dec_late.state = pin(grad_attended, dec_late.state)
    dec_late.near()
    grad_projected = attend_backward(grad_attended, dec_projected, dec_log, all_live, images)
    grad_qkv = narrow(outer_sum(dec_normed, grad_projected))
    grad_projected, grad_qkv, ends = pin(grad_projected, grad_qkv, ends)
    dec_early = scatter_early(grad_qkv, grad_proj)
    ends = ends + swap(ends, 2, devices)
    grad_decoder_in, dec_gain1_grad, dec_bias1_grad = inner_backward(
        grad_middle, grad_projected, decoder_in, vectors[4], vectors[5], dec_qkv_whole
    )
    grad_mask = jnp.sum(jnp.where(live_rows, 0.0, grad_decoder_in), axis=0)
    grad_encoded = jnp.where(live_rows, grad_decoder_in, 0.0)
    grad_encoded, dec_early.state = pin(grad_encoded, dec_early.state)
    dec_early.fold()
    grad_encoded, dec_early.state = pin(grad_encoded, dec_early.state)

    grad_hidden, grad_fc1, grad_fc2 = feed_backward(grad_encoded, enc_feed, enc_fc2_whole)
    grad_hidden, grad_fc1, grad_fc2, dec_late.state, ends = pin(
        grad_hidden, grad_fc1, grad_fc2, dec_late.state, ends
    )
    dec_early.near()
    ends = ends + swap(ends, 4, devices)
    enc_late = scatter_late(grad_fc1, grad_fc2)
    grad_middle, grad_attended, grad_proj, enc_gain2_grad, enc_bias2_grad = middle_backward(
        grad_encoded, grad_hidden, enc_feed, enc_attended, vectors[2], vectors[3], enc_fc1_whole, enc_proj_whole
    )
    grad_attended, grad_proj, enc_late.state = pin(grad_attended, grad_proj, enc_late.state)
    enc_late.fold()
    grad_attended, enc_late.state, dec_early.state, ends = pin(grad_attended, enc_late.state, dec_early.state, ends)
    enc_late.near()
    ends = ends + swap(ends, 8, devices)
    dec_late.far()
    grad_projected = attend_backward(grad_attended, enc_projected, enc_log, live_keys, images)
    grad_qkv = narrow(outer_sum(enc_normed, grad_projected))
    grad_residual, enc_gain1_grad, enc_bias1_grad = inner_backward(
        grad_middle, grad_projected, residual, vectors[0], vectors[1], enc_qkv_whole
    )
    grad_small = [enc_gain1_grad, enc_bias1_grad, enc_gain2_grad, enc_bias2_grad]
    grad_small += [dec_gain1_grad, dec_bias1_grad, dec_gain2_grad, dec_bias2_grad, grad_mask]
    small_count = len(grad_small)
    grad_small = jnp.stack(grad_small).T
    grad_small = jnp.pad(grad_small, ((0, 0), (0, model_width - small_count)))
    grad_residual, grad_qkv, grad_small, dec_late.state, ends = pin(
        grad_residual, grad_qkv, grad_small, dec_late.state, ends
    )
    enc_early = scatter_early(grad_qkv, grad_proj, grad_small)
    rest = 16
    while rest < devices:
        ends = ends + swap(ends, rest, devices)
        rest *= 2
    (enc_early.state,) = pin(enc_early.state)
    enc_early.fold()
    enc_early.state, enc_late.state = pin(enc_early.state, enc_late.state)
    enc_early.near()
    dec_late.along_upper()
    dec_late.state, enc_early.state = pin(dec_late.state, enc_early.state)
    enc_late.far()
    dec_early.far()
    enc_late.state, dec_early.state = pin(enc_late.state, dec_early.state)
    enc_late.along_upper()
    enc_early.far()
    enc_late.state, enc_early.state = pin(enc_late.state, enc_early.state)
    enc_early.along_upper()
    dec_early.along_upper()

    def block_sums(early, late):
        early, late = early.result(), late.result()
        return [from_units(early[:3]), early[3], from_units(late[:fc_count]), late[fc_count:].reshape(-1, model_width)]

    dec_big = block_sums(dec_early, dec_late)
    enc_big = block_sums(enc_early, enc_late)
    me = lax.axis_index("dp")
    inner_rows = diff_out.shape[0]
    loss_sum = ends[2 * CH, 0]
    ends = lax.dynamic_slice_in_dim(ends[: 2 * CH], me * inner_rows, inner_rows, axis=1)
    summed = list(enc_early.result()[4][:, :small_count].T)
    enc_summed = (summed[0], summed[1], enc_big[0], enc_big[1], summed[2], summed[3], enc_big[2], enc_big[3])
    dec_summed = (summed[4], summed[5], dec_big[0], dec_big[1], summed[6], summed[7], dec_big[2], dec_big[3], summed[8])
    diff_summed = (
        ends[:CH],
        mixed[shard_rows:],
        columns_sum(0, 1),
        mixed[:shard_rows],
        columns_sum(3, 6),
        columns_sum(1, 2),
        columns_sum(2, 3),
        columns_sum(6, 8),
        ends[CH:].T,
    )
    loss_mean = loss_sum / count_all
    grad_tokens = grad_residual.reshape(images, positions, model_width)
    return (
        loss_mean,
        grad_tokens,
        enc_summed[0],
        enc_summed[1],
        enc_summed[2],
        enc_summed[3],
        enc_summed[4],
        enc_summed[5],
        enc_summed[6],
        enc_summed[7],
        dec_summed[0],
        dec_summed[1],
        dec_summed[2],
        dec_summed[3],
        dec_summed[4],
        dec_summed[5],
        dec_summed[6],
        dec_summed[7],
        dec_summed[8],
        diff_summed[0],
        diff_summed[1],
        diff_summed[2],
        diff_summed[3],
        diff_summed[4],
        diff_summed[5],
        diff_summed[6],
        diff_summed[7],
        diff_summed[8],
    )


def solution(mesh):
    placed = (
        P("dp", None, None),
        P("dp", None, None),
        P("dp", None),
        P("dp"),
        P("dp", None),
        P("dp", None, None),
        P("dp"),
        P("dp"),
        P("dp", None),
        P("dp", None),
        P("dp"),
        P("dp"),
        P("dp", None),
        P("dp", None),
        P("dp"),
        P("dp"),
        P("dp", None),
        P("dp", None),
        P("dp"),
        P("dp"),
        P("dp", None),
        P("dp", None),
        P("dp"),
        P(None, "dp"),
        P("dp", None),
        P("dp", None),
        P("dp", None),
        P("dp", None),
        P("dp", None),
        P("dp", None),
        P("dp", None),
        P("dp", None),
    )
    return jax.shard_map(
        on_device,
        mesh=mesh,
        in_specs=placed,
        out_specs=(
            P(),
            P("dp", None, None),
            P("dp"),
            P("dp"),
            P("dp", None),
            P("dp", None),
            P("dp"),
            P("dp"),
            P("dp", None),
            P("dp", None),
            P("dp"),
            P("dp"),
            P("dp", None),
            P("dp", None),
            P("dp"),
            P("dp"),
            P("dp", None),
            P("dp", None),
            P("dp"),
            P(None, "dp"),
            P("dp", None),
            P("dp", None),
            P("dp", None),
            P("dp", None),
            P("dp", None),
            P("dp", None),
            P("dp", None),
            P("dp", None),
        ),
        check_vma=False,
    )
```
